32 devices in a mesh: gx: 8 (over z, x), gy: 4 (over y, core).
Axes of the slice: x: 2, y: 2, z: 4, core: 2. Of those that a mesh axis runs over, the one named last changes fastest.
Arguments:
- field: float32 [32, 512, 512], P(None, 'gx', 'gy'), may hold values from -6 to 6
- conductivity: float32 [32, 512, 512], P(None, 'gx', 'gy'), may hold values from 0.2 to 1
- rate: float32 [32, 512, 512], P(None, 'gx', 'gy'), may hold values from 0.05 to 0.5
- patch_cell: int32 [8192], P(('gx', 'gy')), may hold values from 0 to 255
- trainer: int32 [8192, 1], P(('gx', 'gy')), may hold values from 0 to 31; in each aligned block of 256 rows (0 to 255, 256 to 511, ...) at most 16 rows name the same one
- res_slot: int32 [32768], P(('gx', 'gy')), may hold values from 0 to 2047
- reservoir: bfloat16 [65536, 2048], P(('gx', 'gy')), may hold values from -6 to 6
- weights: float32 [2, 1024, 1024], P(None, ('gx', 'gy')), may hold values from -0.1875 to 0.1875
- w_mom: float32 [2, 1024, 1024], P(None, ('gx', 'gy')), may hold values from -0.75 to 0.75
- w_var: float32 [2, 1024, 1024], P(None, ('gx', 'gy')), may hold values from 0.001 to 0.1
- biases: float32 [2, 1024], P(None, ('gx', 'gy')), may hold values from -6 to 6
- b_mom: float32 [2, 1024], P(None, ('gx', 'gy')), may hold values from -0.75 to 0.75
- b_var: float32 [2, 1024], P(None, ('gx', 'gy')), may hold values from 0.001 to 2
Outputs:
- new_field: float32 [32, 512, 512], P(None, 'gx', 'gy')
- new_weights: float32 [2, 1024, 1024], P(None, ('gx', 'gy'))
- new_w_mom: float32 [2, 1024, 1024], P(None, ('gx', 'gy'))
- new_w_var: float32 [2, 1024, 1024], P(None, ('gx', 'gy'))
- new_biases: float32 [2, 1024], P(None, ('gx', 'gy'))
- new_b_mom: float32 [2, 1024], P(None, ('gx', 'gy'))
- new_b_var: float32 [2, 1024], P(None, ('gx', 'gy'))
The draws below stay inside these ranges and needn't reach their ends.
Inputs may be any that keep to these rules, and one draw needn't show every extreme that they name: At most 16 of the patches of one device go to one trainer. `res_slot`: slots of the trainer's own reservoir.
All inputs are finite; a program needn't handle non-finite values.
Results may differ from the reference program's by a relative error of at most 0.0003.
The reference program's roundings to bfloat16 on the way count: a program that leaves them out, or rounds other values in their place, can miss the bound.
Values may be sent and summed in bfloat16 or wider, within the bound.
A program may use at most 128 MiB of HBM per device.

```python
import math
import jax
import jax.numpy as jnp
import numpy as np
from jax import lax

CX = 64
CY = 128
NZ = 32
PW = 32
STEPS = 4
FEAT = 1024
P_DEV = 256
B_OLD = 1024
RES = 2048
CAP = 16
NX = 512
NY = 512
N_GX = 8
N_GY = 4


def place_ends(values, own_key, smallest, top_value):
    extent = values.shape
    place = [jax.random.randint(jax.random.fold_in(own_key, axis), (), 0, extent[axis]) for axis in range(len(extent))]
    values = values.at[tuple(place)].set(smallest)
    longest = extent.index(max(extent))
    place[longest] = (place[longest] + 1) % extent[longest]
    return values.at[tuple(place)].set(top_value)


def block_levels(rng, extent, cuts, low, high):
    def one(dim, parts):
        draws = jax.random.uniform(jax.random.fold_in(jax.random.fold_in(rng, 6), dim), (parts,), jnp.float32, low / len(cuts), high / len(cuts))
        return jnp.repeat(jnp.exp(draws), extent[dim] // parts).reshape((-1,) + (1,) * (len(extent) - dim - 1))

    level = one(*cuts[0])
    for cut in cuts[1:]:
        level = level * one(*cut)
    return level


def routed_block(stream_key, own, number, rows, count, top, most, slope):
    order = jax.random.permutation(stream_key, count)
    packed, common = load_shares(count, rows * top, most, slope, True), load_shares(count, rows * top, most, slope, False)
    places = jnp.arange(count)

    def named(sizes, rotation):
        used = int((sizes > 0).sum())
        fixed = max(1, used // 4)
        moved = fixed + (places - fixed + rotation * (used - fixed)) % max(1, count - fixed)
        return jnp.zeros((count,), jnp.int32).at[order[jnp.where(places < fixed, places, moved)]].set(jnp.asarray(sizes, jnp.int32))

    sizes = jnp.where(number % 4 == 0, named(packed, number // 4), named(common, number - number // 4 - 1))
    mixed = jax.random.permutation(jax.random.fold_in(own, 3), count)
    giver, sink = mixed[0:count // 2 * 2:2], mixed[1:count // 2 * 2:2]
    room = jnp.minimum(sizes[giver] - 1, most - sizes[sink]) // 2
    room = jnp.where((giver == order[0]) | (sink == order[0]) | (sizes[sink] == 0), 0, jnp.maximum(room, 0))
    moved = jax.random.randint(jax.random.fold_in(own, 4), (count // 2,), 0, 1 << 20) % (room + 1)
    sizes = sizes.at[giver].add(-moved).at[sink].add(moved)
    labels = jnp.searchsorted(jnp.cumsum(sizes), jnp.arange(rows * top), side="right").astype(jnp.int32)
    table = labels.reshape(top, rows).T
    table = table[jax.random.permutation(jax.random.fold_in(own, 1), rows)]
    rotation = jax.random.randint(jax.random.fold_in(own, 2), (rows, 1), 0, top)
    return jnp.take_along_axis(table, (jnp.arange(top)[None, :] + rotation) % top, axis=1)


def load_shares(number_of, total, bound, lean, full):
    portions = [(1 << 20) // math.isqrt(rank ** lean) + 1 for rank in range(1, number_of + 1)]
    largest = bound if full else min(bound, max(-(-total // number_of), total * portions[0] // sum(portions)))
    least = 1 if total - largest >= number_of - 1 else 0
    holding, spare = [largest] + [least] * (number_of - 1), total - largest - least * (number_of - 1)
    while spare > 0:
        movable = [i for i in range(1, number_of) if holding[i] < largest] or [i for i in range(1, number_of) if holding[i] < bound]
        pool, budget = sum([portions[i] for i in movable]), spare
        for i in movable:
            extra = min(bound - holding[i], max(1, budget * portions[i] // pool), spare)
            holding[i] = holding[i] + extra
            spare = spare - extra
    return np.array(holding)


def bell_draw(stream_key, dims, scale, reach, split=(), held_as=jnp.bfloat16):
    result = jax.random.normal(stream_key, dims, jnp.float32) * scale
    if len(split) > 0:
        result = block_levels(stream_key, dims, split, -0.22, 0.18) * result
    return jnp.clip(result, min=-reach, max=reach).astype(held_as)


def setup_inputs(seed: int = 0) -> dict:
    splits = jax.random.split(jax.random.key(seed), 14)
    field = bell_draw(splits[0], (NZ, NX, NY), 1.0, 6.0, ((1, 8), (2, 4)), jnp.float32)
    conductivity = jnp.clip(0.2 + 0.8 * jax.random.uniform(splits[1], (NZ, NX, NY), jnp.float32) ** block_levels(splits[1], (NZ, NX, NY), ((1, 8), (2, 4)), -0.2, 0.2), 0.2, 1.0)
    rate = jnp.clip(jnp.exp(math.log(0.5) - 2.3025851 * jax.random.uniform(splits[2], (NZ, NX, NY), jnp.float32) ** block_levels(splits[2], (NZ, NX, NY), ((1, 8), (2, 4)), -0.2, 0.2)), 0.05, 0.5)
    patch_cell = place_ends(jax.random.randint(splits[3], (N_GX * N_GY * P_DEV,), 0, CX * CY // PW), jax.random.fold_in(splits[3], 1), 0, (CX * CY // PW) - 1).astype(jnp.int32)
    trainer_keys = jax.random.split(jax.random.fold_in(splits[4], 1), (N_GX * N_GY * P_DEV) // P_DEV)
    trainer_turns = jax.random.permutation(jax.random.fold_in(splits[4], 3), (N_GX * N_GY * P_DEV) // P_DEV)
    trainer = jax.vmap(lambda own, number: routed_block(jax.random.fold_in(splits[4], 2), own, number, P_DEV, N_GX * N_GY, 1, CAP, 2))(trainer_keys, trainer_turns).reshape((N_GX * N_GY * P_DEV, 1))
    res_slot = place_ends(jax.random.randint(splits[5], (N_GX * N_GY * B_OLD,), 0, RES), jax.random.fold_in(splits[5], 1), 0, RES - 1).astype(jnp.int32)
    reservoir = bell_draw(splits[6], (N_GX * N_GY * RES, 2 * FEAT), 1.0, 6.0, ((0, 32),))
    weights = bell_draw(splits[7], (2, FEAT, FEAT), FEAT ** -0.5, 0.1875, ((1, 32),), jnp.float32)
    w_mom = bell_draw(splits[8], (2, FEAT, FEAT), 0.05, 0.75, ((1, 32),), jnp.float32)
    w_var = jnp.clip(jnp.exp(math.log(0.1) - 4.6051702 * jax.random.uniform(splits[9], (2, FEAT, FEAT), jnp.float32) ** block_levels(splits[9], (2, FEAT, FEAT), ((1, 32),), -0.2, 0.2)), 0.001, 0.1)
    biases = bell_draw(splits[10], (2, FEAT), 0.5, 6.0, ((1, 32),), jnp.float32)
    b_mom = bell_draw(splits[11], (2, FEAT), 0.05, 0.75, ((1, 32),), jnp.float32)
    b_var = jnp.clip(jnp.exp(math.log(2.0) - 7.6009024 * jax.random.uniform(splits[12], (2, FEAT), jnp.float32) ** block_levels(splits[12], (2, FEAT), ((1, 32),), -0.2, 0.2)), 0.001, 2.0)
    return dict(field=field, conductivity=conductivity, rate=rate, patch_cell=patch_cell, trainer=trainer, res_slot=res_slot, reservoir=reservoir, weights=weights, w_mom=w_mom, w_var=w_var, biases=biases, b_mom=b_mom, b_var=b_var)


time_step = 0.15
learn_rate = 0.001
beta_one = 0.9
beta_two = 0.99
adam_count = 20
tiny_eps = 1e-08

def update(padded, kpad, rate_inner):
    inner = slice(1, -1)
    centre = padded[1:-1, 1:-1, 1:-1]
    kcentre = kpad[1:-1, 1:-1, 1:-1]
    sides = [(slice(2, None), inner, inner), (slice(None, -2), inner, inner), (inner, slice(2, None), inner), (inner, slice(None, -2), inner), (inner, inner, slice(2, None)), (inner, inner, slice(None, -2))]
    flux = jnp.zeros_like(centre)
    for where in sides:
        flux = flux + 0.5 * (kcentre + kpad[where]) * (padded[where] - centre)
    return centre + time_step * (flux - rate_inner * centre)

def local_grads(rows, live, wbf, bbf):
    width = wbf.shape[1]
    inputs = rows[:, :width]
    target = rows[:, width:].astype(jnp.float32)
    pre = jnp.dot(inputs, wbf[0], preferred_element_type=jnp.float32) + bbf[0].astype(jnp.float32)
    hidden = jnp.tanh(pre)
    hidden_b = hidden.astype(jnp.bfloat16)
    pred = jnp.dot(hidden_b, wbf[1], preferred_element_type=jnp.float32) + bbf[1].astype(jnp.float32)
    count = jnp.sum(live)
    grad_pred = 2.0 * (pred - target) * live[:, None] / count
    grad_pred_b = grad_pred.astype(jnp.bfloat16)
    grad_w2 = jnp.dot(hidden_b.T, grad_pred_b, preferred_element_type=jnp.float32)
    grad_hid = jnp.dot(grad_pred_b, wbf[1].T, preferred_element_type=jnp.float32)
    grad_pre = grad_hid * (1.0 - hidden * hidden)
    grad_pre_b = grad_pre.astype(jnp.bfloat16)
    grad_w1 = jnp.dot(inputs.T, grad_pre_b, preferred_element_type=jnp.float32)
    return (jnp.stack([grad_w1, grad_w2]), jnp.stack([lax.optimization_barrier(jnp.sum(grad_pre, 0)), lax.optimization_barrier(jnp.sum(grad_pred, 0))]))

def adam(param, moment, second, grad):
    moment_new = beta_one * moment + (1.0 - beta_one) * grad
    second_new = beta_two * second + (1.0 - beta_two) * grad * grad
    mhat = moment_new / (1.0 - beta_one ** adam_count)
    vhat = second_new / (1.0 - beta_two ** adam_count)
    return (param - learn_rate * mhat / (jnp.sqrt(vhat) + tiny_eps), moment_new, second_new)

def reference(field, conductivity, rate, patch_cell, trainer, res_slot, reservoir, weights, w_mom, w_var, biases, b_mom, b_var):
    kpad = jnp.pad(conductivity, 1)
    state = field
    for step in range(STEPS):
        state = update(jnp.pad(state, 1), kpad, rate)
    devices = N_GX * N_GY
    cap = max(2, 2 * P_DEV // devices)
    blocks_y = CY // PW
    total = devices * P_DEV
    gidx = jnp.arange(total, dtype=jnp.int32)
    owner = gidx // P_DEV
    xcell = owner // N_GY * CX + patch_cell // blocks_y
    yblock = owner % N_GY * blocks_y + patch_cell % blocks_y
    stacked = jnp.stack([field, state]).reshape(2, NZ, NX, NY // PW, PW)
    picked = stacked[:, :, xcell, yblock, :]
    patches = jnp.transpose(picked, (2, 0, 1, 3)).reshape(total, 2 * FEAT).astype(jnp.bfloat16)
    target_of = trainer[:, 0]
    onehot = (target_of[:, None] == jnp.arange(devices, dtype=jnp.int32)[None, :]).astype(jnp.int32)
    onehot = onehot.reshape(devices, P_DEV, devices)
    rank = (lax.optimization_barrier(jnp.sum(jnp.cumsum(onehot, 1) * onehot, -1)) - 1).reshape(total)
    dest = (target_of * (devices * cap) + owner * cap + rank).astype(jnp.int32)
    inbox = jnp.zeros((devices * devices * cap, 2 * FEAT), jnp.bfloat16).at[dest].set(patches)
    inbox = inbox.reshape(devices, devices * cap, 2 * FEAT)
    alive = jnp.zeros((devices * devices * cap,), jnp.float32).at[dest].set(1.0).reshape(devices, devices * cap)
    wbf = weights.astype(jnp.bfloat16)
    bbf = biases.astype(jnp.bfloat16)

    def one_trainer(carry, which):
        slots = lax.dynamic_slice_in_dim(res_slot, which * B_OLD, B_OLD)
        store = lax.dynamic_slice_in_dim(reservoir, which * RES, RES, 0)
        rows = jnp.concatenate([store[slots], inbox[which]], 0)
        live = jnp.concatenate([jnp.ones((B_OLD,), jnp.float32), alive[which]])
        grad_w, grad_b = local_grads(rows, live, wbf, bbf)
        return ((carry[0] + grad_w, carry[1] + grad_b), None)
    start = (jnp.zeros(weights.shape, jnp.float32), jnp.zeros(biases.shape, jnp.float32))
    (grad_w, grad_b), unused = lax.scan(one_trainer, start, jnp.arange(devices, dtype=jnp.int32))
    new_w, new_wm, new_wv = adam(weights, w_mom, w_var, grad_w)
    new_b, new_bm, new_bv = adam(biases, b_mom, b_var, grad_b)
    return (state, new_w, new_wm, new_wv, new_b, new_bm, new_bv)
```

```python
import jax
import jax.numpy as jnp
from jax import lax
from jax.sharding import PartitionSpec as P

PW = 32
STEPS = 4


time_step = 0.15
learn_rate = 0.001
beta_one = 0.9
beta_two = 0.99
adam_count = 20
tiny_eps = 1e-08


def with_halo(x, sides, width):
    for axis, dim in sides:
        peers, length = (lax.axis_size(axis), x.shape[dim])
        up = [(i, (i + 1) % peers) for i in range(peers - 1)]
        down = [(j, i) for i, j in up]
        last = lax.slice_in_dim(x, length - width, length, axis=dim)
        first = lax.slice_in_dim(x, 0, width, axis=dim)
        before = lax.ppermute(last, axis, up)
        after = lax.ppermute(first, axis, down)
        x = jnp.concatenate([before, x, after], axis=dim)
    return x


def update(padded, kpad, rate_inner):
    inner = slice(1, -1)
    centre = padded[1:-1, 1:-1, 1:-1]
    kcentre = kpad[1:-1, 1:-1, 1:-1]
    sides = [
        (slice(2, None), inner, inner),
        (slice(None, -2), inner, inner),
        (inner, slice(2, None), inner),
        (inner, slice(None, -2), inner),
        (inner, inner, slice(2, None)),
        (inner, inner, slice(None, -2)),
    ]
    flux = jnp.zeros_like(centre)
    for where in sides:
        flux = flux + 0.5 * (kcentre + kpad[where]) * (padded[where] - centre)
    return centre + time_step * (flux - rate_inner * centre)


def zpad(array):
    return jnp.pad(array, ((1, 1), (0, 0), (0, 0)))


def local_grads(rows, count, wbf, bbf):
    width = wbf[0].shape[1]
    inputs = rows[:, :width]
    target = rows[:, width:].astype(jnp.float32)
    pre = jnp.dot(inputs, wbf[0], preferred_element_type=jnp.float32) + bbf[0].astype(jnp.float32)
    hidden = jnp.tanh(pre)
    hidden_b = hidden.astype(jnp.bfloat16)
    pred = jnp.dot(hidden_b, wbf[1], preferred_element_type=jnp.float32) + bbf[1].astype(
        jnp.float32
    )
    grad_pred = 2.0 * (pred - target) / count[:, None]
    grad_pred_b = grad_pred.astype(jnp.bfloat16)
    grad_w2 = jnp.dot(hidden_b.T, grad_pred_b, preferred_element_type=jnp.float32)
    grad_hid = jnp.dot(grad_pred_b, wbf[1].T, preferred_element_type=jnp.float32)
    grad_pre = grad_hid * (1.0 - hidden * hidden)
    grad_pre_b = grad_pre.astype(jnp.bfloat16)
    grad_w1 = jnp.dot(inputs.T, grad_pre_b, preferred_element_type=jnp.float32)
    return grad_w1, grad_w2, jnp.stack([jnp.sum(grad_pre, 0), jnp.sum(grad_pred, 0)])


def adam(param, moment, second, grad):
    moment_new = beta_one * moment + (1.0 - beta_one) * grad
    second_new = beta_two * second + (1.0 - beta_two) * grad * grad
    mhat = moment_new / (1.0 - beta_one**adam_count)
    vhat = second_new / (1.0 - beta_two**adam_count)
    return (param - learn_rate * mhat / (jnp.sqrt(vhat) + tiny_eps), moment_new, second_new)


def local(
    field,
    conductivity,
    rate,
    patch_cell,
    trainer,
    res_slot,
    reservoir,
    weights,
    w_mom,
    w_var,
    biases,
    b_mom,
    b_var,
):
    depth, cells_x, cells_y = field.shape
    state = field
    kpad = zpad(with_halo(conductivity, (("gx", 1), ("gy", 2)), 1))
    for step in range(STEPS):
        padded = with_halo(state, (("gx", 1), ("gy", 2)), 1)
        state = update(zpad(padded), kpad, rate)
    devices = lax.axis_size("gx") * lax.axis_size("gy")
    count_dev = patch_cell.shape[0]
    stacked = jnp.stack([field, state]).reshape(2, depth, cells_x * cells_y // PW, PW)
    picked = stacked[:, :, patch_cell, :]
    patches = (
        jnp.transpose(picked, (2, 0, 1, 3)).reshape(count_dev, 2 * depth * PW).astype(jnp.bfloat16)
    )
    axes = ("gx", "gy")
    onehot = (trainer == jnp.arange(devices, dtype=jnp.int32)[None, :]).astype(jnp.float32)
    stored = res_slot.shape[0]
    total = stored + lax.psum(jnp.sum(onehot, 0), axes)
    mine = lax.axis_index("gx") * lax.axis_size("gy") + lax.axis_index("gy")
    own = total[mine]
    count = jnp.concatenate(
        [jnp.full((stored,), stored, jnp.float32) - stored + own, jnp.sum(onehot * total, 1)]
    )
    wbf = [lax.all_gather(weights[i].astype(jnp.bfloat16), axes, axis=0, tiled=True) for i in (0, 1)]
    bbf = lax.all_gather(biases.astype(jnp.bfloat16), axes, axis=1, tiled=True)
    rows = jnp.concatenate([reservoir[res_slot], patches], 0)
    grad_1, grad_2, grad_b = local_grads(rows, count, wbf, bbf)
    share_w = jnp.stack(
        [lax.psum_scatter(g, axes, scatter_dimension=0, tiled=True) for g in (grad_1, grad_2)]
    )
    whole_b = lax.psum(grad_b, axes)
    share_b = lax.dynamic_slice_in_dim(whole_b, mine * biases.shape[1], biases.shape[1], 1)
    new_w, new_wm, new_wv = adam(weights, w_mom, w_var, share_w)
    new_b, new_bm, new_bv = adam(biases, b_mom, b_var, share_b)
    return (state, new_w, new_wm, new_wv, new_b, new_bm, new_bv)


def solution(mesh):
    return jax.shard_map(
        local,
        mesh=mesh,
        in_specs=(
            P(None, "gx", "gy"),
            P(None, "gx", "gy"),
            P(None, "gx", "gy"),
            P(("gx", "gy")),
            P(("gx", "gy"), None),
            P(("gx", "gy")),
            P(("gx", "gy"), None),
            P(None, ("gx", "gy"), None),
            P(None, ("gx", "gy"), None),
            P(None, ("gx", "gy"), None),
            P(None, ("gx", "gy")),
            P(None, ("gx", "gy")),
            P(None, ("gx", "gy")),
        ),
        out_specs=(
            P(None, "gx", "gy"),
            P(None, ("gx", "gy"), None),
            P(None, ("gx", "gy"), None),
            P(None, ("gx", "gy"), None),
            P(None, ("gx", "gy")),
            P(None, ("gx", "gy")),
            P(None, ("gx", "gy")),
        ),
        check_vma=False,
    )
```

```python
import functools

import jax
import jax.numpy as jnp
from jax import lax
from jax.experimental import pallas as pl
from jax.experimental.pallas import tpu as pltpu
from jax.sharding import PartitionSpec as P

PW = 32
STEPS = 4
TILE = 256

time_step = 0.15
learn_rate = 0.001
beta_one = 0.9
beta_two = 0.99
adam_count = 20
tiny_eps = 1e-08

MESH = pl.DeviceIdType.MESH
F32 = jnp.float32
BF16 = jnp.bfloat16


def adam(param, moment, second, grad):
    moment_new = beta_one * moment + (1.0 - beta_one) * grad
    second_new = beta_two * second + (1.0 - beta_two) * grad * grad
    mhat = moment_new / (1.0 - beta_one**adam_count)
    vhat = second_new / (1.0 - beta_two**adam_count)
    return (param - learn_rate * mhat / (jnp.sqrt(vhat) + tiny_eps), moment_new, second_new)


def dims_of(gx, gy):
    nx = max(1, gx // 4)
    return (gx // nx, nx, gy // 2, 2)


def kernel(
    gx_n,
    gy_n,
    field,
    cond,
    rate,
    cell,
    trainer,
    slot,
    store,
    w,
    wm,
    wv,
    bias,
    new_field,
    new_w,
    new_wm,
    new_wv,
    bias_grad,
    ua,
    ub,
    coef,
    cz,
    table,
    half,
    rows,
    counts,
    w0,
    w1,
    small,
    hid,
    hidb,
    gpb,
    g0,
    g1,
    brow,
    bsum,
    xsend,
    ysend,
    xrecv,
    yrecv,
    rc0,
    ra0,
    rb0,
    rz0,
    rc1,
    ra1,
    rb1,
    rz1,
    bbuf,
    half_sem,
    hs_sem,
    hr_sem,
    ag_s,
    ag_r,
    rs_s,
    rs_r,
    bs_s,
    bs_r,
):
    dims = dims_of(gx_n, gy_n)
    nz, nx, ny, nc = dims
    gx, gy = lax.axis_index("gx"), lax.axis_index("gy")
    here = (gx // nx, lax.rem(gx, nx), gy // nc, lax.rem(gy, nc))
    depth, cx, cy = field.shape
    width = w.shape[2]

    def device(axis, pos):
        p = list(here)
        p[axis] = pos
        return (p[0] * nx + p[1], p[2] * nc + p[3])

    barrier = pltpu.get_barrier_semaphore()
    for o in range(1, gx_n):
        pl.semaphore_signal(
            barrier, inc=1, device_id=(lax.rem(gx + o, gx_n), gy), device_id_type=MESH
        )
    for o in range(1, gy_n):
        pl.semaphore_signal(
            barrier, inc=1, device_id=(gx, lax.rem(gy + o, gy_n)), device_id_type=MESH
        )

    load = pltpu.make_async_copy(store.at[:, pl.ds(0, width)], half, half_sem.at[0])
    load.start()

    w0[here] = w[0].astype(w0.dtype)
    w1[here] = w[1].astype(w1.dtype)
    devices = gx_n * gy_n
    lane = lax.broadcasted_iota(jnp.int32, (trainer.shape[0], 128), 1)
    hot_t = (trainer[...] == lane).astype(F32)
    sm = jnp.concatenate([jnp.sum(hot_t, 0, keepdims=True), bias[1:8, :]], 0)
    small[here] = sm

    zero_x = jnp.zeros((depth, cy), F32)
    zero_y = jnp.zeros((cx, 128), F32)

    lanes = lax.broadcasted_iota(jnp.int32, (cx, cy), 1)
    subl = lax.broadcasted_iota(jnp.int32, (cx, cy), 0)

    def pack(index, plane):
        def one(z, acc):
            u = plane(z)
            xsend[index, 0, pl.ds(z, 1), :] = u[0:1, :]
            xsend[index, 1, pl.ds(z, 1), :] = u[cx - 1 : cx, :]
            acc = jnp.where(lanes == z, pltpu.roll(u, z, 1), acc)
            return jnp.where(
                lanes == depth + z, pltpu.roll(u, lax.rem(depth + z + 1, cy), 1), acc
            )

        ysend[index] = lax.fori_loop(0, depth, one, jnp.zeros((cx, cy), F32))

    def halo(index):
        out = []
        for side, (axis_pos, n, mk) in enumerate(
            (
                (gx, gx_n, lambda p: (p, gy)),
                (gx, gx_n, lambda p: (p, gy)),
                (gy, gy_n, lambda p: (gx, p)),
                (gy, gy_n, lambda p: (gx, p)),
            )
        ):
            up = side % 2 == 0
            sendbuf = (
                xsend.at[index, 1 if up else 0] if side < 2 else ysend.at[index]
            )
            recvbuf = (xrecv if side < 2 else yrecv).at[index, 0 if up else 1]
            peer = jnp.minimum(axis_pos + 1, n - 1) if up else jnp.maximum(axis_pos - 1, 0)
            copy = pltpu.make_async_remote_copy(
                src_ref=sendbuf,
                dst_ref=recvbuf,
                send_sem=hs_sem.at[index, side],
                recv_sem=hr_sem.at[index, side],
                device_id=mk(peer),
                device_id_type=MESH,
            )
            sends = axis_pos < n - 1 if up else axis_pos > 0
            gets = axis_pos > 0 if up else axis_pos < n - 1
            out.append((copy, sends, gets))
        return out

    def halo_start(index):
        for copy, sends, gets in halo(index):
            pl.when(sends)(copy.start)

    def halo_wait(index):
        for side, (copy, sends, gets) in enumerate(halo(index)):
            pl.when(sends)(copy.wait_send)
            pl.when(gets)(copy.wait_recv)
            buf = xrecv if side < 2 else yrecv

            @pl.when(jnp.logical_not(gets))
            def _():
                buf[index, side % 2] = zero_x if side < 2 else zero_y

    def region(done, fixed=None):
        ind = []
        for a in range(4):
            if fixed is not None and a == fixed[0]:
                ind.append(fixed[1])
            else:
                ind.append(slice(None) if a in done else here[a])
        return tuple(ind)

    def gather(buf, order, which):
        done = []
        for phase, axis in enumerate(order):
            n = dims[axis]
            copies = []
            for o in range(1, n):
                ref = buf.at[region(done)]
                copy = pltpu.make_async_remote_copy(
                    src_ref=ref,
                    dst_ref=ref,
                    send_sem=ag_s.at[which, axis, o - 1],
                    recv_sem=ag_r.at[which, axis, o - 1],
                    device_id=device(axis, lax.rem(here[axis] + o, n)),
                    device_id_type=MESH,
                )
                copy.start()
                copies.append(copy)
            yield
            for copy in copies:
                copy.wait()
            done.append(axis)
            yield

    def step(gens):
        for g in gens:
            next(g, None)

    pack(0, lambda z: cond[z])
    pack(1, lambda z: field[z])
    pl.semaphore_wait(barrier, gx_n - 1 + gy_n - 1)
    halo_start(0)
    halo_start(1)
    gens = [
        gather(small, (0, 1, 2, 3), 0),
        gather(w0, (0, 1, 2, 3), 1),
        gather(w1, (0, 2, 1, 3), 2),
    ]
    step(gens)

    n_old = slot.shape[0]
    n_slots = store.shape[0]

    def pick(col):
        def one(t, carry):
            r = pl.ds(pl.multiple_of(t * TILE, TILE), TILE)
            hot = (
                slot[r, :] == lax.broadcasted_iota(jnp.int32, (TILE, n_slots), 1)
            ).astype(F32).astype(BF16)
            rows[r, pl.ds(col, width)] = jnp.dot(
                hot, half[...], preferred_element_type=F32
            ).astype(BF16)
            return carry

        lax.fori_loop(0, n_old // TILE, one, 0)

    def shifted(u, index, z):
        lo = xrecv[index, 0, pl.ds(z, 1), :]
        hi = xrecv[index, 1, pl.ds(z, 1), :]
        xm = jnp.where(subl == 0, lo, pltpu.roll(u, 1, 0))
        xp = jnp.where(subl == cx - 1, hi, pltpu.roll(u, cx - 1, 0))
        left = pltpu.roll(yrecv[index, 0], lax.rem(2 * cy - depth - z, cy), 1)
        right = pltpu.roll(yrecv[index, 1], cy - 1 - z, 1)
        ym = jnp.where(lanes == 0, left, pltpu.roll(u, 1, 1))
        yp = jnp.where(lanes == cy - 1, right, pltpu.roll(u, cy - 1, 1))
        return xm, xp, ym, yp

    half_step = 0.5 * time_step
    for buf in (ua, ub):
        buf[0] = jnp.zeros((cx, cy), F32)
        buf[depth + 1] = jnp.zeros((cx, cy), F32)
    cz[0] = half_step * cond[0]
    cz[depth] = half_step * cond[depth - 1]

    def z_coef(z, carry):
        cz[z] = half_step * (cond[z - 1] + cond[z])
        return carry

    lax.fori_loop(1, depth, z_coef, 0)
    halo_wait(0)

    def make_coef(z, carry):
        k = cond[z]
        total = time_step * rate[z] + cz[z] + cz[z + 1]
        for i, kn in enumerate(shifted(k, 0, z)):
            c = half_step * (k + kn)
            coef[i, z] = c
            total = total + c
        coef[4, z] = 1.0 - total
        ua[z + 1] = field[z]
        return carry

    lax.fori_loop(0, depth, make_coef, 0)

    def advance(index, src, dst):
        def one(z, carry):
            u = src[z + 1]
            acc = coef[4, z] * u + cz[z] * src[z] + cz[z + 1] * src[z + 2]
            for i, un in enumerate(shifted(u, index, z)):
                acc = acc + coef[i, z] * un
            dst[z + 1] = acc
            return carry

        lax.fori_loop(0, depth, one, 0)

    load.wait()
    pick(0)
    load2 = pltpu.make_async_copy(store.at[:, pl.ds(width, width)], half, half_sem.at[1])
    load2.start()
    step(gens)
    step(gens)

    halo_wait(1)
    bufs = (ua, ub)
    for s in range(STEPS):
        src, dst = bufs[s % 2], bufs[(s + 1) % 2]
        advance(s + 1, src, dst)
        if s < STEPS - 1:
            pack(s + 2, lambda z: dst[z + 1])
            halo_start(s + 2)
            if s == 0:
                load2.wait()
                pick(width)
            if s == 1:
                step(gens)
                step(gens)
            halo_wait(s + 2)
    last = bufs[STEPS % 2]

    blocks = cy // PW
    per = 128 // PW
    group = lanes // PW

    def build(offset, plane):
        def one(q, carry):
            planes = [plane(q * per + j) for j in range(per)]
            for b in range(blocks):
                acc = None
                for j in range(per):
                    shift = (PW * (j - b)) % cy
                    v = planes[j] if shift == 0 else pltpu.roll(planes[j], shift, 1)
                    acc = v if acc is None else jnp.where(group == j, v, acc)
                table[
                    b * cx : (b + 1) * cx,
                    pl.ds(pl.multiple_of(offset + q * 128, 128), 128),
                ] = acc.astype(BF16)
            return carry

        lax.fori_loop(0, depth // per, one, 0)

    build(0, lambda z: field[z])
    build(width, lambda z: last[z + 1])

    def emit(z, carry):
        new_field[z] = last[z + 1]
        return carry

    lax.fori_loop(0, depth, emit, 0)
    n_new = cell.shape[0]
    n_cells = table.shape[0]
    hot_c = (
        (cell[...] == lax.broadcasted_iota(jnp.int32, (n_new, n_cells), 1))
        .astype(F32)
        .astype(BF16)
    )
    for c in range(0, 2 * width, 512):
        rows[n_old : n_old + n_new, c : c + 512] = jnp.dot(
            hot_c, table[:, c : c + 512], preferred_element_type=F32
        ).astype(BF16)

    step(gens)
    step(gens)
    step(gens)

    everyone = small[...].reshape(devices, 8, 128)
    totals = jnp.sum(everyone[:, 0, :], 0, keepdims=True) + float(n_old)
    position = gx * gy_n + gy
    lane1 = lax.broadcasted_iota(jnp.int32, (1, 128), 1)
    mine = jnp.sum(jnp.where(lane1 == position, totals, 0.0), 1, keepdims=True)
    counts[0:n_old, :] = jnp.broadcast_to(mine, (n_old, 128))
    counts[n_old : n_old + n_new, :] = jnp.broadcast_to(
        jnp.sum(hot_t * totals, 1, keepdims=True), (n_new, 128)
    )
    share = width // devices
    fit = 128 // share
    for layer in range(2):
        for j in range(width // 128):
            acc = jnp.zeros((1, 128), F32)
            for i in range(fit):
                acc = jnp.where(lane1 // share == i, everyone[j * fit + i, layer + 1 : layer + 2, :], acc)
            brow[layer : layer + 1, j * 128 : (j + 1) * 128] = acc.astype(BF16).astype(F32)

    n_rows = n_old + n_new
    bsum[...] = jnp.zeros_like(bsum)

    def whole(ref):
        return ref[...].astype(BF16).reshape(width, width)

    def forward(t, carry):
        r = pl.ds(pl.multiple_of(t * TILE, TILE), TILE)
        pre = jnp.dot(rows[r, :width], whole(w0), preferred_element_type=F32) + brow[0:1, :]
        h = jnp.tanh(pre)
        hid[r, :] = h
        hidb[r, :] = h.astype(BF16)
        return carry

    lax.fori_loop(0, n_rows // TILE, forward, 0)

    def forward2(t, carry):
        r = pl.ds(pl.multiple_of(t * TILE, TILE), TILE)
        pred = jnp.dot(hidb[r, :], whole(w1), preferred_element_type=F32) + brow[1:2, :]
        gp = 2.0 * (pred - rows[r, width : 2 * width].astype(F32)) / counts[r, 0:1]
        gpb[r, :] = gp.astype(BF16)
        bsum[1:2, :] += jnp.sum(gp, 0, keepdims=True)
        return carry

    lax.fori_loop(0, n_rows // TILE, forward2, 0)

    def reduce(buf, order, stages, which):
        left = [0, 1, 2, 3]
        for phase, axis in enumerate(order):
            n = dims[axis]
            stage = stages[phase]
            copies = []
            for o in range(1, n):
                peer = lax.rem(here[axis] + o, n)
                copy = pltpu.make_async_remote_copy(
                    src_ref=buf.at[region(left, (axis, peer))],
                    dst_ref=stage.at[o - 1],
                    send_sem=rs_s.at[which, axis, o - 1],
                    recv_sem=rs_r.at[which, axis, o - 1],
                    device_id=device(axis, peer),
                    device_id_type=MESH,
                )
                copy.start()
                copies.append(copy)
            yield
            left.remove(axis)
            own = region(left)
            for o, copy in enumerate(copies):
                copy.wait()
            shape = [dims[a] for a in range(4) if a in left]

            def total(i, carry):
                ind, sub, rest = [], [], i
                for a in reversed(left):
                    ind.insert(0, lax.rem(rest, dims[a]))
                    rest = rest // dims[a]
                full = list(here)
                for a, v in zip(left, ind):
                    full[a] = v
                acc = buf[tuple(full)]
                for o in range(n - 1):
                    acc = acc + stage[(o, *ind)]
                buf[tuple(full)] = acc
                return carry

            count = 1
            for m in shape:
                count *= m
            if count == 1:
                total(0, 0)
            else:
                lax.fori_loop(0, count, total, 0)
            yield

    def reduce_bias():
        for phase, axis in enumerate((3, 2, 1, 0)):
            n = dims[axis]
            copies = []
            for o in range(1, n):
                copy = pltpu.make_async_remote_copy(
                    src_ref=bbuf.at[axis, 0],
                    dst_ref=bbuf.at[axis, o],
                    send_sem=bs_s.at[axis, o - 1],
                    recv_sem=bs_r.at[axis, o - 1],
                    device_id=device(axis, lax.rem(here[axis] + o, n)),
                    device_id_type=MESH,
                )
                copy.start()
                copies.append(copy)
            yield
            for copy in copies:
                copy.wait()
            acc = bbuf[axis, 0]
            for o in range(1, n):
                acc = acc + bbuf[axis, o]
            if axis > 0:
                bbuf[axis - 1, 0] = acc
            else:
                bias_grad[...] = acc
            yield

    across = (((0,), (0,)), ((), ()))

    def store_grad(buf, col, value):
        per_tile = TILE // share
        flat = value.reshape(per_tile, share, width)

        for i in range(per_tile):
            d = col * per_tile + i
            buf[
                d // (nx * ny * nc),
                lax.rem(d // (ny * nc), nx),
                lax.rem(d // nc, ny),
                lax.rem(d, nc),
            ] = flat[i]

    def grad_two(j, carry):
        c = pl.ds(pl.multiple_of(j * TILE, TILE), TILE)
        store_grad(
            g1, j, lax.dot_general(hidb[:, c], gpb[...], across, preferred_element_type=F32)
        )
        return carry

    lax.fori_loop(0, width // TILE, grad_two, 0)
    red1 = reduce(g1, (3, 1, 2, 0), (rc1, ra1, rb1, rz1), 1)
    next(red1)

    def backward(t, carry):
        r = pl.ds(pl.multiple_of(t * TILE, TILE), TILE)
        gh = lax.dot_general(
            gpb[r, :], whole(w1), (((1,), (1,)), ((), ())), preferred_element_type=F32
        )
        h = hid[r, :]
        ga = gh * (1.0 - h * h)
        hidb[r, :] = ga.astype(BF16)
        bsum[0:1, :] += jnp.sum(ga, 0, keepdims=True)
        return carry

    lax.fori_loop(0, n_rows // TILE, backward, 0)
    bbuf[3, 0] = bsum[...]
    redb = reduce_bias()
    next(redb)
    next(red1)
    next(red1)

    def grad_one(j, carry):
        c = pl.ds(pl.multiple_of(j * TILE, TILE), TILE)
        store_grad(
            g0, j, lax.dot_general(rows[:, c], hidb[...], across, preferred_element_type=F32)
        )
        return carry

    lax.fori_loop(0, width // TILE, grad_one, 0)
    red0 = reduce(g0, (3, 2, 1, 0), (rc0, rb0, ra0, rz0), 0)
    next(red0)
    for _ in range(2):
        next(redb, None)
    for _ in range(3):
        step([red0, red0])
        step([red1, red1])
        step([redb, redb])

    def finish(layer, buf):
        p, m, v = adam(w[layer], wm[layer], wv[layer], buf[here])
        new_w[layer] = p
        new_wm[layer] = m
        new_wv[layer] = v

    step([red1])
    finish(1, g1)
    step([red0])
    finish(0, g0)
    step([redb, redb])


def local(
    field,
    conductivity,
    rate,
    patch_cell,
    trainer,
    res_slot,
    reservoir,
    weights,
    w_mom,
    w_var,
    biases,
    b_mom,
    b_var,
):
    gx_n, gy_n = lax.axis_size("gx"), lax.axis_size("gy")
    devices = gx_n * gy_n
    dims = dims_of(gx_n, gy_n)
    nz, nx, ny, nc = dims
    depth, cx, cy = field.shape
    share, width = weights.shape[1], weights.shape[2]
    blocks = cy // PW
    n_old, n_new = res_slot.shape[0], patch_cell.shape[0]
    n_rows = n_old + n_new
    cell = ((patch_cell % blocks) * cx + patch_cell // blocks)[:, None]
    slot = res_slot[:, None]
    wide = jnp.tile(biases, (1, 128 // share))
    bias8 = jnp.concatenate([jnp.zeros((1, 128), F32), wide, jnp.zeros((5, 128), F32)], 0)
    wire = BF16 if share % 16 == 0 else F32
    most = max(dims) - 1
    full = (*dims, share, width)
    vm = pl.BlockSpec(memory_space=pltpu.VMEM)
    shard = jax.ShapeDtypeStruct(weights.shape, F32)

    def scratch(*shape, dtype=F32):
        return pltpu.VMEM(shape, dtype)

    dma = pltpu.SemaphoreType.DMA
    out = pl.pallas_call(
        functools.partial(kernel, gx_n, gy_n),
        out_shape=(
            jax.ShapeDtypeStruct(field.shape, F32),
            shard,
            shard,
            shard,
            jax.ShapeDtypeStruct((8, width), F32),
        ),
        in_specs=[vm] * 6 + [pl.BlockSpec(memory_space=pl.ANY)] + [vm] * 4,
        out_specs=[vm] * 5,
        scratch_shapes=[
            scratch(depth + 2, cx, cy),
            scratch(depth + 2, cx, cy),
            scratch(5, depth, cx, cy),
            scratch(depth + 1, cx, cy),
            scratch(blocks * cx, 2 * width, dtype=BF16),
            scratch(reservoir.shape[0], width, dtype=BF16),
            scratch(n_rows, 2 * width, dtype=BF16),
            scratch(n_rows, 128),
            scratch(*full, dtype=wire),
            scratch(*full, dtype=wire),
            scratch(*dims, 8, 128),
            scratch(n_rows, width),
            scratch(n_rows, width, dtype=BF16),
            scratch(n_rows, width, dtype=BF16),
            scratch(*full),
            scratch(*full),
            scratch(8, width),
            scratch(8, width),
            scratch(STEPS + 1, 2, depth, cy),
            scratch(STEPS + 1, cx, cy),
            scratch(STEPS + 1, 2, depth, cy),
            scratch(STEPS + 1, 2, cx, cy),
            scratch(nc - 1, nz, nx, ny, share, width),
            scratch(nx - 1, nz, share, width),
            scratch(ny - 1, nz, nx, share, width),
            scratch(nz - 1, share, width),
            scratch(nc - 1, nz, nx, ny, share, width),
            scratch(nx - 1, nz, ny, share, width),
            scratch(ny - 1, nz, share, width),
            scratch(nz - 1, share, width),
            scratch(4, most + 1, 8, width),
            dma((2,)),
            dma((STEPS + 1, 4)),
            dma((STEPS + 1, 4)),
            dma((3, 4, most)),
            dma((3, 4, most)),
            dma((2, 4, most)),
            dma((2, 4, most)),
            dma((4, most)),
            dma((4, most)),
        ],
        compiler_params=pltpu.CompilerParams(
            collective_id=0, has_side_effects=True, vmem_limit_bytes=62 * 2**20
        ),
        cost_estimate=pl.CostEstimate(
            flops=10 * n_rows * width * width, bytes_accessed=32 * 2**20, transcendentals=0
        ),
    )(field, conductivity, rate, cell, trainer, slot, reservoir, weights, w_mom, w_var, bias8)
    state, new_w, new_wm, new_wv, bias_grad = out
    position = lax.axis_index("gx") * gy_n + lax.axis_index("gy")
    share_b = lax.dynamic_slice_in_dim(bias_grad[:2], position * share, share, 1)
    new_b, new_bm, new_bv = adam(biases, b_mom, b_var, share_b)
    return (state, new_w, new_wm, new_wv, new_b, new_bm, new_bv)


def solution(mesh):
    return jax.shard_map(
        local,
        mesh=mesh,
        in_specs=(
            P(None, "gx", "gy"),
            P(None, "gx", "gy"),
            P(None, "gx", "gy"),
            P(("gx", "gy")),
            P(("gx", "gy"), None),
            P(("gx", "gy")),
            P(("gx", "gy"), None),
            P(None, ("gx", "gy"), None),
            P(None, ("gx", "gy"), None),
            P(None, ("gx", "gy"), None),
            P(None, ("gx", "gy")),
            P(None, ("gx", "gy")),
            P(None, ("gx", "gy")),
        ),
        out_specs=(
            P(None, "gx", "gy"),
            P(None, ("gx", "gy"), None),
            P(None, ("gx", "gy"), None),
            P(None, ("gx", "gy"), None),
            P(None, ("gx", "gy")),
            P(None, ("gx", "gy")),
            P(None, ("gx", "gy")),
        ),
        check_vma=False,
    )
```

```python
import functools

import jax
import jax.numpy as jnp
from jax import lax
from jax.experimental import pallas as pl
from jax.experimental.pallas import tpu as pltpu
from jax.sharding import PartitionSpec as P

PW = 32
STEPS = 4
TILE = 256

time_step = 0.15
learn_rate = 0.001
beta_one = 0.9
beta_two = 0.99
adam_count = 20
tiny_eps = 1e-08

MESH = pl.DeviceIdType.MESH
F32 = jnp.float32
BF16 = jnp.bfloat16


def adam(param, moment, second, grad):
    moment_new = beta_one * moment + (1.0 - beta_one) * grad
    second_new = beta_two * second + (1.0 - beta_two) * grad * grad
    mhat = moment_new / (1.0 - beta_one**adam_count)
    vhat = second_new / (1.0 - beta_two**adam_count)
    return (param - learn_rate * mhat / (jnp.sqrt(vhat) + tiny_eps), moment_new, second_new)


def dims_of(gx, gy):
    nx = max(1, gx // 4)
    return (gx // nx, nx, gy // 2, 2)


def kernel(
    gx_n,
    gy_n,
    field,
    cond,
    rate,
    ids,
    store,
    w,
    bias,
    new_field,
    grad_out,
    bias_grad,
    slot,
    cell,
    trainer,
    tiny,
    ua,
    ub,
    coef,
    cz,
    table,
    half,
    rows,
    counts,
    w0,
    w1,
    small,
    hid,
    gpb,
    g0,
    g1,
    brow,
    bsum,
    xsend,
    ysend,
    xrecv,
    yrecv,
    stages0,
    stages1,
    bbuf,
    half_sem,
    hs_sem,
    hr_sem,
    ag_s,
    ag_r,
    rs_s,
    rs_r,
    bs_s,
    bs_r,
):
    dims = dims_of(gx_n, gy_n)
    nz, nx, ny, nc = dims
    gx, gy = lax.axis_index("gx"), lax.axis_index("gy")
    here = (gx // nx, lax.rem(gx, nx), gy // nc, lax.rem(gy, nc))
    depth, cx, cy = field.shape
    width = w.shape[2]
    hidb = half.at[pl.ds(0, rows.shape[0])]

    def loop(count, body, together):
        def several(q, carry):
            for j in range(together):
                body(q * together + j)
            return carry

        lax.fori_loop(0, count // together, several, 0)

    def device(axis, pos):
        p = list(here)
        p[axis] = pos
        return (p[0] * nx + p[1], p[2] * nc + p[3])

    barrier = pltpu.get_barrier_semaphore()
    for o in range(1, gx_n):
        pl.semaphore_signal(
            barrier, inc=1, device_id=(lax.rem(gx + o, gx_n), gy), device_id_type=MESH
        )
    for o in range(1, gy_n):
        pl.semaphore_signal(
            barrier, inc=1, device_id=(gx, lax.rem(gy + o, gy_n)), device_id_type=MESH
        )

    load = pltpu.make_async_copy(store.at[:, pl.ds(0, width)], half, half_sem.at[0])
    load.start()

    w0[here] = w[0].astype(w0.dtype)
    w1[here] = w[1].astype(w1.dtype)
    devices = gx_n * gy_n
    share = w.shape[1]
    upright = jnp.transpose(ids[...])
    place = 0
    for ref in (slot, cell, trainer):
        for g in range(ref.shape[0] // 128):
            ref[g * 128 : (g + 1) * 128, :] = jnp.broadcast_to(
                upright[:, place : place + 1], (128, 128)
            )
            place += 1
    lane = lax.broadcasted_iota(jnp.int32, trainer.shape, 1)
    hot_t = (trainer[...] == lane).astype(F32)
    tiny[...] = jnp.zeros_like(tiny)
    tiny[1:3, 0:share] = bias[...]
    sm = tiny[...]
    for i in range(1, 128 // share):
        sm = sm + pltpu.roll(tiny[...], share * i, 1)
    small[here] = sm
    small[(*here, pl.ds(0, 1))] = jnp.sum(hot_t, 0, keepdims=True)

    zero_x = jnp.zeros((depth, cy), F32)
    zero_y = jnp.zeros((cx, 128), F32)

    lanes = lax.broadcasted_iota(jnp.int32, (cx, cy), 1)
    subl = lax.broadcasted_iota(jnp.int32, (cx, cy), 0)

    def pack(index, plane):
        def several(q, acc):
            for j in range(8):
                z = q * 8 + j
                u = plane(z)
                xsend[index, 0, pl.ds(z, 1), :] = u[0:1, :]
                xsend[index, 1, pl.ds(z, 1), :] = u[cx - 1 : cx, :]
                acc = jnp.where(lanes == z, pltpu.roll(u, z, 1), acc)
                acc = jnp.where(
                    lanes == depth + z, pltpu.roll(u, lax.rem(depth + z + 1, cy), 1), acc
                )
            return acc

        ysend[index] = lax.fori_loop(0, depth // 8, several, jnp.zeros((cx, cy), F32))

    def halo(index):
        out = []
        for side, (axis_pos, n, mk) in enumerate(
            (
                (gx, gx_n, lambda p: (p, gy)),
                (gx, gx_n, lambda p: (p, gy)),
                (gy, gy_n, lambda p: (gx, p)),
                (gy, gy_n, lambda p: (gx, p)),
            )
        ):
            up = side % 2 == 0
            sendbuf = (
                xsend.at[index, 1 if up else 0] if side < 2 else ysend.at[index]
            )
            recvbuf = (xrecv if side < 2 else yrecv).at[index, 0 if up else 1]
            peer = jnp.minimum(axis_pos + 1, n - 1) if up else jnp.maximum(axis_pos - 1, 0)
            copy = pltpu.make_async_remote_copy(
                src_ref=sendbuf,
                dst_ref=recvbuf,
                send_sem=hs_sem.at[index, side],
                recv_sem=hr_sem.at[index, side],
                device_id=mk(peer),
                device_id_type=MESH,
            )
            sends = axis_pos < n - 1 if up else axis_pos > 0
            gets = axis_pos > 0 if up else axis_pos < n - 1
            out.append((copy, sends, gets))
        return out

    def halo_start(index):
        for copy, sends, gets in halo(index):
            pl.when(sends)(copy.start)

    def halo_wait(index):
        for side, (copy, sends, gets) in enumerate(halo(index)):
            pl.when(sends)(copy.wait_send)
            pl.when(gets)(copy.wait_recv)
            buf = xrecv if side < 2 else yrecv

            @pl.when(jnp.logical_not(gets))
            def _():
                buf[index, side % 2] = zero_x if side < 2 else zero_y

    def region(done, fixed=None):
        ind = []
        for a in range(4):
            if fixed is not None and a == fixed[0]:
                ind.append(fixed[1])
            else:
                ind.append(slice(None) if a in done else here[a])
        return tuple(ind)

    def gather(buf, order, which):
        done = []
        for phase, axis in enumerate(order):
            n = dims[axis]
            copies = []
            for o in range(1, n):
                ref = buf.at[region(done)]
                copy = pltpu.make_async_remote_copy(
                    src_ref=ref,
                    dst_ref=ref,
                    send_sem=ag_s.at[which, axis, o - 1],
                    recv_sem=ag_r.at[which, axis, o - 1],
                    device_id=device(axis, lax.rem(here[axis] + o, n)),
                    device_id_type=MESH,
                )
                copy.start()
                copies.append(copy)
            yield
            for copy in copies:
                copy.wait()
            done.append(axis)
            yield

    def step(gens):
        for g in gens:
            next(g, None)

    pl.semaphore_wait(barrier, gx_n - 1 + gy_n - 1)
    gens = [
        gather(small, (0, 1, 2, 3), 0),
        gather(w0, (0, 1, 2, 3), 1),
        gather(w1, (0, 2, 1, 3), 2),
    ]
    step(gens)
    pack(0, lambda z: cond[z])
    halo_start(0)
    pack(1, lambda z: field[z])
    halo_start(1)

    n_old = slot.shape[0]
    n_slots = store.shape[0]

    def pick(col, first, last):
        def one(t, carry):
            r = pl.ds(pl.multiple_of(t * TILE, TILE), TILE)
            hot = (
                slot[r, 0:1] == lax.broadcasted_iota(jnp.int32, (TILE, n_slots), 1)
            ).astype(F32).astype(BF16)
            rows[r, pl.ds(col, width)] = jnp.dot(
                hot, half[...], preferred_element_type=F32
            ).astype(BF16)
            return carry

        tiles = n_old // TILE
        lax.fori_loop(tiles * first // 2, tiles * last // 2, one, 0)

    def shifted(u, index, z):
        lo = xrecv[index, 0, pl.ds(z, 1), :]
        hi = xrecv[index, 1, pl.ds(z, 1), :]
        xm = jnp.where(subl == 0, lo, pltpu.roll(u, 1, 0))
        xp = jnp.where(subl == cx - 1, hi, pltpu.roll(u, cx - 1, 0))
        left = pltpu.roll(yrecv[index, 0], lax.rem(2 * cy - depth - z, cy), 1)
        right = pltpu.roll(yrecv[index, 1], cy - 1 - z, 1)
        ym = jnp.where(lanes == 0, left, pltpu.roll(u, 1, 1))
        yp = jnp.where(lanes == cy - 1, right, pltpu.roll(u, cy - 1, 1))
        return xm, xp, ym, yp

    half_step = 0.5 * time_step
    for buf in (ua, ub):
        buf[0] = jnp.zeros((cx, cy), F32)
        buf[depth + 1] = jnp.zeros((cx, cy), F32)
    cz[0] = half_step * cond[0]
    cz[depth] = half_step * cond[depth - 1]

    def z_coef(z):
        cz[z] = half_step * (cond[z - 1] + cond[z])
        ua[z] = field[z - 1]

    loop(depth - 1, lambda z: z_coef(z + 1), 1)
    ua[depth] = field[depth - 1]
    load.wait()
    pick(0, 0, 1)
    halo_wait(0)

    def make_coef(z):
        k = cond[z]
        total = time_step * rate[z] + cz[z] + cz[z + 1]
        for i, kn in enumerate(shifted(k, 0, z)):
            c = half_step * (k + kn)
            coef[i, z] = c
            total = total + c
        coef[4, z] = 1.0 - total

    loop(depth, make_coef, 4)

    def advance(index, src, dst):
        def one(z):
            u = src[z + 1]
            acc = coef[4, z] * u + cz[z] * src[z] + cz[z + 1] * src[z + 2]
            for i, un in enumerate(shifted(u, index, z)):
                acc = acc + coef[i, z] * un
            dst[z + 1] = acc

        loop(depth, one, 4)

    pick(0, 1, 2)
    load2 = pltpu.make_async_copy(store.at[:, pl.ds(width, width)], half, half_sem.at[1])
    load2.start()
    step(gens)
    step(gens)

    blocks = cy // PW
    per = 128 // PW
    group = lanes // PW

    def build(offset, plane):
        def one(q, carry):
            planes = [plane(q * per + j) for j in range(per)]
            for b in range(blocks):
                acc = None
                for j in range(per):
                    shift = (PW * (j - b)) % cy
                    v = planes[j] if shift == 0 else pltpu.roll(planes[j], shift, 1)
                    acc = v if acc is None else jnp.where(group == j, v, acc)
                table[
                    b * cx : (b + 1) * cx,
                    pl.ds(pl.multiple_of(offset + q * 128, 128), 128),
                ] = acc.astype(BF16)
            return carry

        lax.fori_loop(0, depth // per, one, 0)

    halo_wait(1)
    bufs = (ua, ub)
    for s in range(STEPS):
        src, dst = bufs[s % 2], bufs[(s + 1) % 2]
        advance(s + 1, src, dst)
        if s < STEPS - 1:
            pack(s + 2, lambda z: dst[z + 1])
            halo_start(s + 2)
            if s == 0:
                load2.wait()
                pick(width, 0, 1)
            if s == 1:
                pick(width, 1, 2)
                step(gens)
                step(gens)
            if s == 2:
                build(0, lambda z: field[z])
            halo_wait(s + 2)
    last = bufs[STEPS % 2]

    build(width, lambda z: last[z + 1])

    def emit(z):
        new_field[z] = last[z + 1]

    loop(depth, emit, 4)
    n_new = cell.shape[0]
    n_cells = table.shape[0]
    hot_c = (
        (cell[:, 0:1] == lax.broadcasted_iota(jnp.int32, (n_new, n_cells), 1))
        .astype(F32)
        .astype(BF16)
    )
    for c in range(0, 2 * width, 512):
        rows[n_old : n_old + n_new, c : c + 512] = jnp.dot(
            hot_c, table[:, c : c + 512], preferred_element_type=F32
        ).astype(BF16)

    step(gens)
    step(gens)
    step(gens)

    everyone = small[...].reshape(devices, 8, 128)
    totals = jnp.sum(everyone[:, 0, :], 0, keepdims=True) + float(n_old)
    position = gx * gy_n + gy
    lane1 = lax.broadcasted_iota(jnp.int32, (1, 128), 1)
    mine = jnp.sum(jnp.where(lane1 == position, totals, 0.0), 1, keepdims=True)
    counts[0:n_old, :] = jnp.broadcast_to(mine, (n_old, 128))
    counts[n_old : n_old + n_new, :] = jnp.broadcast_to(
        jnp.sum(hot_t * totals, 1, keepdims=True), (n_new, 128)
    )
    fit = 128 // share
    for layer in range(2):
        for j in range(width // 128):
            acc = jnp.zeros((1, 128), F32)
            for i in range(fit):
                acc = jnp.where(lane1 // share == i, everyone[j * fit + i, layer + 1 : layer + 2, :], acc)
            brow[layer : layer + 1, j * 128 : (j + 1) * 128] = acc.astype(BF16).astype(F32)

    n_rows = n_old + n_new
    tall = 640 if n_rows % 640 == 0 else TILE
    bsum[...] = jnp.zeros_like(bsum)

    def whole(ref):
        return ref[...].astype(BF16).reshape(width, width)

    def forward(t, carry):
        r = pl.ds(pl.multiple_of(t * tall, tall), tall)
        pre = jnp.dot(rows[r, :width], whole(w0), preferred_element_type=F32) + brow[0:1, :]
        h = jnp.tanh(pre)
        hid[r, :] = h
        hidb[r, :] = h.astype(BF16)
        return carry

    lax.fori_loop(0, n_rows // tall, forward, 0)

    def forward2(t, carry):
        r = pl.ds(pl.multiple_of(t * tall, tall), tall)
        pred = jnp.dot(hidb[r, :], whole(w1), preferred_element_type=F32) + brow[1:2, :]
        gp = 2.0 * (pred - rows[r, width : 2 * width].astype(F32)) / counts[r, 0:1]
        gpb[r, :] = gp.astype(BF16)
        bsum[1:2, :] += jnp.sum(gp, 0, keepdims=True)
        return carry

    lax.fori_loop(0, n_rows // tall, forward2, 0)

    coded = share % 16 == 0

    def each(left, body):
        count = 1
        for a in left:
            count *= dims[a]

        def one(i, carry):
            ind, rest = [], i
            for a in reversed(left):
                ind.insert(0, lax.rem(rest, dims[a]))
                rest = rest // dims[a]
            full = list(here)
            for a, v in zip(left, ind):
                full[a] = v
            body(full, ind)
            return carry

        if count == 1:
            one(0, 0)
        else:
            lax.fori_loop(0, count, one, 0)

    def reduce(buf, order, stages, which):
        left = [0, 1, 2, 3]
        for phase, axis in enumerate(order):
            n = dims[axis]
            others = [a for a in left if a != axis]
            out, got, out_scale, got_scale = stages[phase]
            copies = []
            for o in range(1, n):
                peer = lax.rem(here[axis] + o, n)
                pairs = [(buf.at[region(left, (axis, peer))], got.at[o - 1])]
                if coded:

                    def encode(full, ind):
                        full[axis] = peer
                        v = buf[tuple(full)]
                        top = jnp.max(jnp.abs(v), axis=0, keepdims=True)
                        top = jnp.maximum(jnp.max(top, axis=1, keepdims=True), 1e-30)
                        q = jnp.round(v * (32767.0 / top))
                        out[(o - 1, *ind)] = q.astype(jnp.int32).astype(jnp.int16)
                        out_scale[(o - 1, *ind)] = jnp.broadcast_to(top / 32767.0, (8, 128))

                    each(others, encode)
                    pairs = [
                        (out.at[o - 1], got.at[o - 1]),
                        (out_scale.at[o - 1], got_scale.at[o - 1]),
                    ]
                for part, (src, dst) in enumerate(pairs):
                    copy = pltpu.make_async_remote_copy(
                        src_ref=src,
                        dst_ref=dst,
                        send_sem=rs_s.at[which, axis, o - 1, part],
                        recv_sem=rs_r.at[which, axis, o - 1, part],
                        device_id=device(axis, peer),
                        device_id_type=MESH,
                    )
                    copy.start()
                    copies.append(copy)
            yield
            left.remove(axis)
            for copy in copies:
                copy.wait()

            def total(full, ind):
                acc = buf[tuple(full)]
                for o in range(n - 1):
                    v = got[(o, *ind)]
                    if coded:
                        v = v.astype(jnp.int32).astype(F32) * got_scale[(o, *ind)][0:1, 0:1]
                    acc = acc + v
                buf[tuple(full)] = acc

            each(left, total)
            yield

    def reduce_bias():
        for phase, axis in enumerate((3, 2, 1, 0)):
            n = dims[axis]
            copies = []
            for o in range(1, n):
                copy = pltpu.make_async_remote_copy(
                    src_ref=bbuf.at[axis, 0],
                    dst_ref=bbuf.at[axis, o],
                    send_sem=bs_s.at[axis, o - 1],
                    recv_sem=bs_r.at[axis, o - 1],
                    device_id=device(axis, lax.rem(here[axis] + o, n)),
                    device_id_type=MESH,
                )
                copy.start()
                copies.append(copy)
            yield
            for copy in copies:
                copy.wait()
            acc = bbuf[axis, 0]
            for o in range(1, n):
                acc = acc + bbuf[axis, o]
            if axis > 0:
                bbuf[axis - 1, 0] = acc
            else:
                bias_grad[...] = acc
            yield

    across = (((0,), (0,)), ((), ()))

    def store_grad(buf, col, value):
        per_tile = TILE // share
        flat = value.reshape(per_tile, share, width)

        for i in range(per_tile):
            d = col * per_tile + i
            buf[
                d // (nx * ny * nc),
                lax.rem(d // (ny * nc), nx),
                lax.rem(d // nc, ny),
                lax.rem(d, nc),
            ] = flat[i]

    def grad_two(j, carry):
        c = pl.ds(pl.multiple_of(j * TILE, TILE), TILE)
        store_grad(
            g1, j, lax.dot_general(hidb[:, c], gpb[...], across, preferred_element_type=F32)
        )
        return carry

    lax.fori_loop(0, width // TILE, grad_two, 0)
    red1 = reduce(g1, (3, 1, 2, 0), stages1, 1)
    next(red1)

    def backward(t, carry):
        r = pl.ds(pl.multiple_of(t * tall, tall), tall)
        gh = lax.dot_general(
            gpb[r, :], whole(w1), (((1,), (1,)), ((), ())), preferred_element_type=F32
        )
        h = hid[r, :]
        ga = gh * (1.0 - h * h)
        hidb[r, :] = ga.astype(BF16)
        bsum[0:1, :] += jnp.sum(ga, 0, keepdims=True)
        return carry

    lax.fori_loop(0, n_rows // tall, backward, 0)
    bbuf[3, 0] = bsum[...]
    redb = reduce_bias()
    next(redb)
    next(red1)
    next(red1)

    def grad_one(j, carry):
        c = pl.ds(pl.multiple_of(j * TILE, TILE), TILE)
        store_grad(
            g0, j, lax.dot_general(rows[:, c], hidb[...], across, preferred_element_type=F32)
        )
        return carry

    lax.fori_loop(0, width // TILE, grad_one, 0)
    red0 = reduce(g0, (3, 2, 1, 0), stages0, 0)
    next(red0)
    for _ in range(2):
        next(redb, None)
    for _ in range(3):
        step([red0, red0])
        step([red1, red1])
        step([redb, redb])

    step([red1])
    grad_out[1] = g1[here]
    step([red0])
    grad_out[0] = g0[here]
    step([redb, redb])


def local(
    field,
    conductivity,
    rate,
    patch_cell,
    trainer,
    res_slot,
    reservoir,
    weights,
    w_mom,
    w_var,
    biases,
    b_mom,
    b_var,
):
    gx_n, gy_n = lax.axis_size("gx"), lax.axis_size("gy")
    devices = gx_n * gy_n
    dims = dims_of(gx_n, gy_n)
    nz, nx, ny, nc = dims
    depth, cx, cy = field.shape
    share, width = weights.shape[1], weights.shape[2]
    blocks = cy // PW
    n_old, n_new = res_slot.shape[0], patch_cell.shape[0]
    n_rows = n_old + n_new
    cell = (patch_cell % blocks) * cx + patch_cell // blocks
    ids = jnp.concatenate([res_slot, cell, trainer[:, 0]]).reshape(-1, 128)
    ids = jnp.pad(ids, ((0, -ids.shape[0] % 8), (0, 0)))
    wire = BF16 if share % 16 == 0 else F32
    most = max(dims) - 1
    full = (*dims, share, width)
    vm = pl.BlockSpec(memory_space=pltpu.VMEM)

    def scratch(*shape, dtype=F32):
        return pltpu.VMEM(shape, dtype)

    coded = share % 16 == 0

    def stages(order):
        left, found = [0, 1, 2, 3], []
        for axis in order:
            left.remove(axis)
            shape = (dims[axis] - 1, *(dims[a] for a in left))
            body = (*shape, share, width) if coded else (1,) * (len(shape) + 2)
            scale = (*shape, 8, 128) if coded else (1,) * (len(shape) + 2)
            kind = jnp.int16 if coded else F32
            found.append(
                (
                    scratch(*body, dtype=kind),
                    scratch(*shape, share, width, dtype=kind),
                    scratch(*scale),
                    scratch(*scale),
                )
            )
        return tuple(found)

    dma = pltpu.SemaphoreType.DMA
    out = pl.pallas_call(
        functools.partial(kernel, gx_n, gy_n),
        out_shape=(
            jax.ShapeDtypeStruct(field.shape, F32),
            jax.ShapeDtypeStruct(weights.shape, F32),
            jax.ShapeDtypeStruct((8, width), F32),
        ),
        in_specs=[vm] * 4 + [pl.BlockSpec(memory_space=pl.ANY)] + [vm] * 2,
        out_specs=[vm] * 3,
        scratch_shapes=[
            scratch(n_old, 128, dtype=jnp.int32),
            scratch(n_new, 128, dtype=jnp.int32),
            scratch(n_new, 128, dtype=jnp.int32),
            scratch(8, 128),
            scratch(depth + 2, cx, cy),
            scratch(depth + 2, cx, cy),
            scratch(5, depth, cx, cy),
            scratch(depth + 1, cx, cy),
            scratch(blocks * cx, 2 * width, dtype=BF16),
            scratch(reservoir.shape[0], width, dtype=BF16),
            scratch(n_rows, 2 * width, dtype=BF16),
            scratch(n_rows, 128),
            scratch(*full, dtype=wire),
            scratch(*full, dtype=wire),
            scratch(*dims, 8, 128),
            scratch(n_rows, width),
            scratch(n_rows, width, dtype=BF16),
            scratch(*full),
            scratch(*full),
            scratch(8, width),
            scratch(8, width),
            scratch(STEPS + 1, 2, depth, cy),
            scratch(STEPS + 1, cx, cy),
            scratch(STEPS + 1, 2, depth, cy),
            scratch(STEPS + 1, 2, cx, cy),
            stages((3, 2, 1, 0)),
            stages((3, 1, 2, 0)),
            scratch(4, most + 1, 8, width),
            dma((2,)),
            dma((STEPS + 1, 4)),
            dma((STEPS + 1, 4)),
            dma((3, 4, most)),
            dma((3, 4, most)),
            dma((2, 4, most, 2)),
            dma((2, 4, most, 2)),
            dma((4, most)),
            dma((4, most)),
        ],
        compiler_params=pltpu.CompilerParams(
            collective_id=0, has_side_effects=True, vmem_limit_bytes=62 * 2**20
        ),
        cost_estimate=pl.CostEstimate(
            flops=10 * n_rows * width * width, bytes_accessed=32 * 2**20, transcendentals=0
        ),
    )(field, conductivity, rate, ids, reservoir, weights, biases)
    state, share_w, bias_grad = out
    new_w, new_wm, new_wv = adam(weights, w_mom, w_var, share_w)
    position = lax.axis_index("gx") * gy_n + lax.axis_index("gy")
    share_b = lax.dynamic_slice_in_dim(bias_grad[:2], position * share, share, 1)
    new_b, new_bm, new_bv = adam(biases, b_mom, b_var, share_b)
    return (state, new_w, new_wm, new_wv, new_b, new_bm, new_bv)


def solution(mesh):
    return jax.shard_map(
        local,
        mesh=mesh,
        in_specs=(
            P(None, "gx", "gy"),
            P(None, "gx", "gy"),
            P(None, "gx", "gy"),
            P(("gx", "gy")),
            P(("gx", "gy"), None),
            P(("gx", "gy")),
            P(("gx", "gy"), None),
            P(None, ("gx", "gy"), None),
            P(None, ("gx", "gy"), None),
            P(None, ("gx", "gy"), None),
            P(None, ("gx", "gy")),
            P(None, ("gx", "gy")),
            P(None, ("gx", "gy")),
        ),
        out_specs=(
            P(None, "gx", "gy"),
            P(None, ("gx", "gy"), None),
            P(None, ("gx", "gy"), None),
            P(None, ("gx", "gy"), None),
            P(None, ("gx", "gy")),
            P(None, ("gx", "gy")),
            P(None, ("gx", "gy")),
        ),
        check_vma=False,
    )
```

```python
import functools

import jax
import jax.numpy as jnp
from jax import lax
from jax.experimental import pallas as pl
from jax.experimental.pallas import tpu as pltpu
from jax.sharding import PartitionSpec as P

PW = 32
STEPS = 4
TILE = 256

time_step = 0.15
learn_rate = 0.001
beta_one = 0.9
beta_two = 0.99
adam_count = 20
tiny_eps = 1e-08

MESH = pl.DeviceIdType.MESH
F32 = jnp.float32
BF16 = jnp.bfloat16


def adam(param, moment, second, grad):
    moment_new = beta_one * moment + (1.0 - beta_one) * grad
    second_new = beta_two * second + (1.0 - beta_two) * grad * grad
    mhat = moment_new / (1.0 - beta_one**adam_count)
    vhat = second_new / (1.0 - beta_two**adam_count)
    return (param - learn_rate * mhat / (jnp.sqrt(vhat) + tiny_eps), moment_new, second_new)


def dims_of(gx, gy):
    nx = max(1, gx // 4)
    return (gx // nx, nx, gy // 2, 2)


def kernel(
    gx_n,
    gy_n,
    field,
    cond,
    rate,
    ids,
    store,
    w,
    bias,
    new_field,
    grad_out,
    bias_grad,
    slot,
    cell,
    trainer,
    tiny,
    ua,
    ub,
    coef,
    cz,
    table,
    half,
    rows,
    counts,
    w0,
    w1,
    small,
    hid,
    gpb,
    g0,
    g1,
    brow,
    bsum,
    xsend,
    ysend,
    xrecv,
    yrecv,
    stages,
    bbuf,
    half_sem,
    hs_sem,
    hr_sem,
    ag_s,
    ag_r,
    rs_s,
    rs_r,
    bs_s,
    bs_r,
):
    dims = dims_of(gx_n, gy_n)
    nz, nx, ny, nc = dims
    gx, gy = lax.axis_index("gx"), lax.axis_index("gy")
    here = (gx // nx, lax.rem(gx, nx), gy // nc, lax.rem(gy, nc))
    depth, cx, cy = field.shape
    width = w.shape[2]
    hidb = half.at[pl.ds(0, rows.shape[0])]

    def loop(count, body, together):
        def several(q, carry):
            for j in range(together):
                body(q * together + j)
            return carry

        lax.fori_loop(0, count // together, several, 0)

    def device(axis, pos):
        p = list(here)
        p[axis] = pos
        return (p[0] * nx + p[1], p[2] * nc + p[3])

    barrier = pltpu.get_barrier_semaphore()
    for o in range(1, gx_n):
        pl.semaphore_signal(
            barrier, inc=1, device_id=(lax.rem(gx + o, gx_n), gy), device_id_type=MESH
        )
    for o in range(1, gy_n):
        pl.semaphore_signal(
            barrier, inc=1, device_id=(gx, lax.rem(gy + o, gy_n)), device_id_type=MESH
        )

    load = pltpu.make_async_copy(store.at[:, pl.ds(0, width)], half, half_sem.at[0])
    load.start()

    w0[here] = w[0].astype(w0.dtype)
    w1[here] = w[1].astype(w1.dtype)
    devices = gx_n * gy_n
    share = w.shape[1]
    upright = jnp.transpose(ids[...])
    place = 0
    for ref in (slot, cell, trainer):
        for g in range(ref.shape[0] // 128):
            ref[g * 128 : (g + 1) * 128, :] = jnp.broadcast_to(
                upright[:, place : place + 1], (128, 128)
            )
            place += 1
    lane = lax.broadcasted_iota(jnp.int32, trainer.shape, 1)
    hot_t = (trainer[...] == lane).astype(F32)
    tiny[...] = jnp.zeros_like(tiny)
    tiny[1:3, 0:share] = bias[...]
    sm = tiny[...]
    for i in range(1, 128 // share):
        sm = sm + pltpu.roll(tiny[...], share * i, 1)
    small[here] = sm
    small[(*here, pl.ds(0, 1))] = jnp.sum(hot_t, 0, keepdims=True)

    zero_x = jnp.zeros((depth, cy), F32)
    zero_y = jnp.zeros((cx, 128), F32)

    lanes = lax.broadcasted_iota(jnp.int32, (cx, cy), 1)
    subl = lax.broadcasted_iota(jnp.int32, (cx, cy), 0)

    def pack(index, plane):
        def several(q, acc):
            for j in range(8):
                z = q * 8 + j
                u = plane(z)
                xsend[index, 0, pl.ds(z, 1), :] = u[0:1, :]
                xsend[index, 1, pl.ds(z, 1), :] = u[cx - 1 : cx, :]
                acc = jnp.where(lanes == z, pltpu.roll(u, z, 1), acc)
                acc = jnp.where(
                    lanes == depth + z, pltpu.roll(u, lax.rem(depth + z + 1, cy), 1), acc
                )
            return acc

        ysend[index] = lax.fori_loop(0, depth // 8, several, jnp.zeros((cx, cy), F32))

    def halo(index):
        out = []
        for side, (axis_pos, n, mk) in enumerate(
            (
                (gx, gx_n, lambda p: (p, gy)),
                (gx, gx_n, lambda p: (p, gy)),
                (gy, gy_n, lambda p: (gx, p)),
                (gy, gy_n, lambda p: (gx, p)),
            )
        ):
            up = side % 2 == 0
            sendbuf = (
                xsend.at[index, 1 if up else 0] if side < 2 else ysend.at[index]
            )
            recvbuf = (xrecv if side < 2 else yrecv).at[index, 0 if up else 1]
            peer = jnp.minimum(axis_pos + 1, n - 1) if up else jnp.maximum(axis_pos - 1, 0)
            copy = pltpu.make_async_remote_copy(
                src_ref=sendbuf,
                dst_ref=recvbuf,
                send_sem=hs_sem.at[index, side],
                recv_sem=hr_sem.at[index, side],
                device_id=mk(peer),
                device_id_type=MESH,
            )
            sends = axis_pos < n - 1 if up else axis_pos > 0
            gets = axis_pos > 0 if up else axis_pos < n - 1
            out.append((copy, sends, gets))
        return out

    def halo_start(index):
        for copy, sends, gets in halo(index):
            pl.when(sends)(copy.start)

    def halo_wait(index):
        for side, (copy, sends, gets) in enumerate(halo(index)):
            pl.when(sends)(copy.wait_send)
            pl.when(gets)(copy.wait_recv)
            buf = xrecv if side < 2 else yrecv

            @pl.when(jnp.logical_not(gets))
            def _():
                buf[index, side % 2] = zero_x if side < 2 else zero_y

    def region(done, fixed=None):
        ind = []
        for a in range(4):
            if fixed is not None and a == fixed[0]:
                ind.append(fixed[1])
            else:
                ind.append(slice(None) if a in done else here[a])
        return tuple(ind)

    def gather(buf, order, which):
        done = []
        for phase, axis in enumerate(order):
            n = dims[axis]
            copies = []
            for o in range(1, n):
                ref = buf.at[region(done)]
                copy = pltpu.make_async_remote_copy(
                    src_ref=ref,
                    dst_ref=ref,
                    send_sem=ag_s.at[which, axis, o - 1],
                    recv_sem=ag_r.at[which, axis, o - 1],
                    device_id=device(axis, lax.rem(here[axis] + o, n)),
                    device_id_type=MESH,
                )
                copy.start()
                copies.append(copy)
            yield
            for copy in copies:
                copy.wait()
            done.append(axis)
            yield

    def step(gens):
        for g in gens:
            next(g, None)

    pl.semaphore_wait(barrier, gx_n - 1 + gy_n - 1)
    gens = [
        gather(small, (0, 1, 2, 3), 0),
        gather(w0, (0, 1, 2, 3), 1),
        gather(w1, (0, 2, 1, 3), 2),
    ]
    step(gens)
    pack(0, lambda z: cond[z])
    halo_start(0)
    pack(1, lambda z: field[z])
    halo_start(1)

    n_old = slot.shape[0]
    n_slots = store.shape[0]

    pick_tile = 512 if n_old % 1024 == 0 else TILE

    def pick(col, first, last):
        def one(t, carry):
            r = pl.ds(pl.multiple_of(t * pick_tile, pick_tile), pick_tile)
            hot = (
                slot[r, 0:1] == lax.broadcasted_iota(jnp.int32, (pick_tile, n_slots), 1)
            ).astype(F32).astype(BF16)
            rows[r, pl.ds(col, width)] = jnp.dot(
                hot, half[...], preferred_element_type=F32
            ).astype(BF16)
            return carry

        tiles = n_old // pick_tile
        lax.fori_loop(tiles * first // 2, tiles * last // 2, one, 0)

    def shifted(u, index, z):
        lo = xrecv[index, 0, pl.ds(z, 1), :]
        hi = xrecv[index, 1, pl.ds(z, 1), :]
        xm = jnp.where(subl == 0, lo, pltpu.roll(u, 1, 0))
        xp = jnp.where(subl == cx - 1, hi, pltpu.roll(u, cx - 1, 0))
        left = pltpu.roll(yrecv[index, 0], lax.rem(2 * cy - depth - z, cy), 1)
        right = pltpu.roll(yrecv[index, 1], cy - 1 - z, 1)
        ym = jnp.where(lanes == 0, left, pltpu.roll(u, 1, 1))
        yp = jnp.where(lanes == cy - 1, right, pltpu.roll(u, cy - 1, 1))
        return xm, xp, ym, yp

    half_step = 0.5 * time_step
    for buf in (ua, ub):
        buf[0] = jnp.zeros((cx, cy), F32)
        buf[depth + 1] = jnp.zeros((cx, cy), F32)
    cz[0] = half_step * cond[0]
    cz[depth] = half_step * cond[depth - 1]

    def z_coef(z):
        cz[z] = half_step * (cond[z - 1] + cond[z])
        ua[z] = field[z - 1]

    loop(depth - 1, lambda z: z_coef(z + 1), 1)
    ua[depth] = field[depth - 1]
    load.wait()
    pick(0, 0, 1)
    halo_wait(0)

    def make_coef(z):
        k = cond[z]
        total = time_step * rate[z] + cz[z] + cz[z + 1]
        for i, kn in enumerate(shifted(k, 0, z)):
            c = half_step * (k + kn)
            coef[i, z] = c
            total = total + c
        coef[4, z] = 1.0 - total

    loop(depth, make_coef, 4)

    def advance(index, src, dst):
        def one(z):
            u = src[z + 1]
            acc = coef[4, z] * u + cz[z] * src[z] + cz[z + 1] * src[z + 2]
            for i, un in enumerate(shifted(u, index, z)):
                acc = acc + coef[i, z] * un
            dst[z + 1] = acc

        loop(depth, one, 4)

    step(gens)
    step(gens)
    pick(0, 1, 2)
    load2 = pltpu.make_async_copy(store.at[:, pl.ds(width, width)], half, half_sem.at[1])
    load2.start()

    blocks = cy // PW
    per = 128 // PW
    group = lanes // PW

    def build(offset, plane):
        def one(q, carry):
            planes = [plane(q * per + j) for j in range(per)]
            for b in range(blocks):
                acc = None
                for j in range(per):
                    shift = (PW * (j - b)) % cy
                    v = planes[j] if shift == 0 else pltpu.roll(planes[j], shift, 1)
                    acc = v if acc is None else jnp.where(group == j, v, acc)
                table[
                    b * cx : (b + 1) * cx,
                    pl.ds(pl.multiple_of(offset + q * 128, 128), 128),
                ] = acc.astype(BF16)
            return carry

        lax.fori_loop(0, depth // per, one, 0)

    halo_wait(1)
    bufs = (ua, ub)
    for s in range(STEPS):
        src, dst = bufs[s % 2], bufs[(s + 1) % 2]
        advance(s + 1, src, dst)
        if s < STEPS - 1:
            pack(s + 2, lambda z: dst[z + 1])
            halo_start(s + 2)
            if s == 0:
                load2.wait()
                pick(width, 0, 1)
                step(gens)
                step(gens)
            if s == 1:
                pick(width, 1, 2)
            if s == 2:
                build(0, lambda z: field[z])
                step(gens)
                step(gens)
            halo_wait(s + 2)
    last = bufs[STEPS % 2]

    build(width, lambda z: last[z + 1])

    def emit(z):
        new_field[z] = last[z + 1]

    loop(depth, emit, 4)
    n_new = cell.shape[0]
    n_cells = table.shape[0]
    hot_c = (
        (cell[:, 0:1] == lax.broadcasted_iota(jnp.int32, (n_new, n_cells), 1))
        .astype(F32)
        .astype(BF16)
    )
    for c in range(0, 2 * width, 512):
        rows[n_old : n_old + n_new, c : c + 512] = jnp.dot(
            hot_c, table[:, c : c + 512], preferred_element_type=F32
        ).astype(BF16)

    step(gens)

    everyone = small[...].reshape(devices, 8, 128)
    totals = jnp.sum(everyone[:, 0, :], 0, keepdims=True) + float(n_old)
    position = gx * gy_n + gy
    lane1 = lax.broadcasted_iota(jnp.int32, (1, 128), 1)
    mine = jnp.sum(jnp.where(lane1 == position, totals, 0.0), 1, keepdims=True)
    counts[0:n_old, :] = jnp.broadcast_to(mine, (n_old, 128))
    counts[n_old : n_old + n_new, :] = jnp.broadcast_to(
        jnp.sum(hot_t * totals, 1, keepdims=True), (n_new, 128)
    )
    fit = 128 // share
    for layer in range(2):
        for j in range(width // 128):
            acc = jnp.zeros((1, 128), F32)
            for i in range(fit):
                acc = jnp.where(lane1 // share == i, everyone[j * fit + i, layer + 1 : layer + 2, :], acc)
            brow[layer : layer + 1, j * 128 : (j + 1) * 128] = acc.astype(BF16).astype(F32)

    n_rows = n_old + n_new
    tall = 640 if n_rows % 640 == 0 else TILE
    bsum[...] = jnp.zeros_like(bsum)

    def whole(ref):
        return ref[...].astype(BF16).reshape(width, width)

    def forward(t, carry):
        r = pl.ds(pl.multiple_of(t * tall, tall), tall)
        pre = jnp.dot(rows[r, :width], whole(w0), preferred_element_type=F32) + brow[0:1, :]
        h = jnp.tanh(pre)
        hid[r, :] = h
        hidb[r, :] = h.astype(BF16)
        return carry

    lax.fori_loop(0, n_rows // tall, forward, 0)

    def forward2(t, carry):
        r = pl.ds(pl.multiple_of(t * tall, tall), tall)
        pred = jnp.dot(hidb[r, :], whole(w1), preferred_element_type=F32) + brow[1:2, :]
        gp = 2.0 * (pred - rows[r, width : 2 * width].astype(F32)) / counts[r, 0:1]
        gpb[r, :] = gp.astype(BF16)
        bsum[1:2, :] += jnp.sum(gp, 0, keepdims=True)
        return carry

    lax.fori_loop(0, n_rows // tall, forward2, 0)

    coded = share % 16 == 0

    def each(left, body):
        count = 1
        for a in left:
            count *= dims[a]

        def one(i):
            ind, rest = [], i
            for a in reversed(left):
                ind.insert(0, lax.rem(rest, dims[a]))
                rest = rest // dims[a]
            full = list(here)
            for a, v in zip(left, ind):
                full[a] = v
            body(full, ind)

        if count <= 4:
            for i in range(count):
                one(i)
        else:
            loop(count, one, 4 if count % 4 == 0 else 1)

    def reduce(buf, piece, order):
        left = [0, 1, 2, 3]
        stage = stages[piece]
        cols = (slice(None), pl.ds(piece % 2 * (width // 2), width // 2))
        for phase, axis in enumerate(order):
            n = dims[axis]
            others = [a for a in left if a != axis]
            out, got, out_scale, got_scale = stage[phase]
            copies = []
            for o in range(1, n):
                peer = lax.rem(here[axis] + o, n)
                pairs = [(buf.at[(*region(left, (axis, peer)), *cols)], got.at[o - 1])]
                if coded:

                    def encode(full, ind):
                        full[axis] = peer
                        v = buf[(*full, *cols)]
                        top = jnp.max(jnp.abs(v), axis=0, keepdims=True)
                        top = jnp.maximum(jnp.max(top, axis=1, keepdims=True), 1e-30)
                        q = jnp.round(v * (32767.0 / top))
                        out[(o - 1, *ind)] = q.astype(jnp.int32).astype(jnp.int16)
                        out_scale[(o - 1, *ind)] = jnp.broadcast_to(top / 32767.0, (8, 128))

                    each(others, encode)
                    pairs = [
                        (out.at[o - 1], got.at[o - 1]),
                        (out_scale.at[o - 1], got_scale.at[o - 1]),
                    ]
                for part, (src, dst) in enumerate(pairs):
                    copy = pltpu.make_async_remote_copy(
                        src_ref=src,
                        dst_ref=dst,
                        send_sem=rs_s.at[piece, axis, o - 1, part],
                        recv_sem=rs_r.at[piece, axis, o - 1, part],
                        device_id=device(axis, peer),
                        device_id_type=MESH,
                    )
                    copy.start()
                    copies.append(copy)
            yield
            left.remove(axis)
            for copy in copies:
                copy.wait()

            def total(full, ind):
                acc = buf[(*full, *cols)]
                for o in range(n - 1):
                    v = got[(o, *ind)]
                    if coded:
                        v = v.astype(jnp.int32).astype(F32) * got_scale[(o, *ind)][0:1, 0:1]
                    acc = acc + v
                buf[(*full, *cols)] = acc

            each(left, total)
            yield

    def reduce_bias():
        for phase, axis in enumerate((3, 2, 1, 0)):
            n = dims[axis]
            copies = []
            for o in range(1, n):
                copy = pltpu.make_async_remote_copy(
                    src_ref=bbuf.at[axis, 0],
                    dst_ref=bbuf.at[axis, o],
                    send_sem=bs_s.at[axis, o - 1],
                    recv_sem=bs_r.at[axis, o - 1],
                    device_id=device(axis, lax.rem(here[axis] + o, n)),
                    device_id_type=MESH,
                )
                copy.start()
                copies.append(copy)
            yield
            for copy in copies:
                copy.wait()
            acc = bbuf[axis, 0]
            for o in range(1, n):
                acc = acc + bbuf[axis, o]
            if axis > 0:
                bbuf[axis - 1, 0] = acc
            else:
                bias_grad[...] = acc
            yield

    across = (((0,), (0,)), ((), ()))

    def store_grad(buf, col, value):
        per_tile = TILE // share
        flat = value.reshape(per_tile, share, width)

        for i in range(per_tile):
            d = col * per_tile + i
            buf[
                d // (nx * ny * nc),
                lax.rem(d // (ny * nc), nx),
                lax.rem(d // nc, ny),
                lax.rem(d, nc),
            ] = flat[i]

    def grad_two(j, carry):
        c = pl.ds(pl.multiple_of(j * TILE, TILE), TILE)
        store_grad(
            g1, j, lax.dot_general(hidb[:, c], gpb[...], across, preferred_element_type=F32)
        )
        return carry

    lax.fori_loop(0, width // TILE, grad_two, 0)
    layer1 = [reduce(g1, 2, (3, 1, 2, 0)), reduce(g1, 3, (3, 2, 1, 0))]
    layer0 = [reduce(g0, 0, (3, 1, 2, 0)), reduce(g0, 1, (3, 2, 1, 0))]

    def onward(pieces):
        for piece in pieces:
            step([piece, piece])

    step(layer1)

    def backward(t, carry):
        r = pl.ds(pl.multiple_of(t * tall, tall), tall)
        gh = lax.dot_general(
            gpb[r, :], whole(w1), (((1,), (1,)), ((), ())), preferred_element_type=F32
        )
        h = hid[r, :]
        ga = gh * (1.0 - h * h)
        hidb[r, :] = ga.astype(BF16)
        bsum[0:1, :] += jnp.sum(ga, 0, keepdims=True)
        return carry

    tiles = n_rows // tall
    lax.fori_loop(0, tiles // 2, backward, 0)
    onward(layer1)
    lax.fori_loop(tiles // 2, tiles, backward, 0)
    bbuf[3, 0] = bsum[...]
    redb = reduce_bias()
    next(redb)

    def grad_one(j, carry):
        c = pl.ds(pl.multiple_of(j * TILE, TILE), TILE)
        store_grad(
            g0, j, lax.dot_general(rows[:, c], hidb[...], across, preferred_element_type=F32)
        )
        return carry

    lax.fori_loop(0, width // TILE // 2, grad_one, 0)
    onward(layer1)
    onward([redb])
    lax.fori_loop(width // TILE // 2, width // TILE, grad_one, 0)
    step(layer0)
    onward(layer1)
    onward([redb])
    onward(layer0)
    onward([redb])
    onward(layer0)
    onward([redb])
    step(layer1)
    grad_out[1] = g1[here]
    onward(layer0)
    step(layer0)
    grad_out[0] = g0[here]


def local(
    field,
    conductivity,
    rate,
    patch_cell,
    trainer,
    res_slot,
    reservoir,
    weights,
    w_mom,
    w_var,
    biases,
    b_mom,
    b_var,
):
    gx_n, gy_n = lax.axis_size("gx"), lax.axis_size("gy")
    devices = gx_n * gy_n
    dims = dims_of(gx_n, gy_n)
    nz, nx, ny, nc = dims
    depth, cx, cy = field.shape
    share, width = weights.shape[1], weights.shape[2]
    blocks = cy // PW
    n_old, n_new = res_slot.shape[0], patch_cell.shape[0]
    n_rows = n_old + n_new
    cell = (patch_cell % blocks) * cx + patch_cell // blocks
    ids = jnp.concatenate([res_slot, cell, trainer[:, 0]]).reshape(-1, 128)
    ids = jnp.pad(ids, ((0, -ids.shape[0] % 8), (0, 0)))
    wire = BF16 if share % 16 == 0 else F32
    most = max(dims) - 1
    full = (*dims, share, width)
    vm = pl.BlockSpec(memory_space=pltpu.VMEM)

    def scratch(*shape, dtype=F32):
        return pltpu.VMEM(shape, dtype)

    coded = share % 16 == 0

    def stages(order):
        left, found = [0, 1, 2, 3], []
        for axis in order:
            left.remove(axis)
            shape = (dims[axis] - 1, *(dims[a] for a in left))
            body = (*shape, share, width // 2) if coded else (1,) * (len(shape) + 2)
            scale = (*shape, 8, 128) if coded else (1,) * (len(shape) + 2)
            kind = jnp.int16 if coded else F32
            found.append(
                (
                    scratch(*body, dtype=kind),
                    scratch(*shape, share, width // 2, dtype=kind),
                    scratch(*scale),
                    scratch(*scale),
                )
            )
        return tuple(found)

    dma = pltpu.SemaphoreType.DMA
    out = pl.pallas_call(
        functools.partial(kernel, gx_n, gy_n),
        out_shape=(
            jax.ShapeDtypeStruct(field.shape, F32),
            jax.ShapeDtypeStruct(weights.shape, F32),
            jax.ShapeDtypeStruct((8, width), F32),
        ),
        in_specs=[vm] * 4 + [pl.BlockSpec(memory_space=pl.ANY)] + [vm] * 2,
        out_specs=[vm] * 3,
        scratch_shapes=[
            scratch(n_old, 128, dtype=jnp.int32),
            scratch(n_new, 128, dtype=jnp.int32),
            scratch(n_new, 128, dtype=jnp.int32),
            scratch(8, 128),
            scratch(depth + 2, cx, cy),
            scratch(depth + 2, cx, cy),
            scratch(5, depth, cx, cy),
            scratch(depth + 1, cx, cy),
            scratch(blocks * cx, 2 * width, dtype=BF16),
            scratch(reservoir.shape[0], width, dtype=BF16),
            scratch(n_rows, 2 * width, dtype=BF16),
            scratch(n_rows, 128),
            scratch(*full, dtype=wire),
            scratch(*full, dtype=wire),
            scratch(*dims, 8, 128),
            scratch(n_rows, width),
            scratch(n_rows, width, dtype=BF16),
            scratch(*full),
            scratch(*full),
            scratch(8, width),
            scratch(8, width),
            scratch(STEPS + 1, 2, depth, cy),
            scratch(STEPS + 1, cx, cy),
            scratch(STEPS + 1, 2, depth, cy),
            scratch(STEPS + 1, 2, cx, cy),
            tuple(stages(order) for order in ((3, 1, 2, 0), (3, 2, 1, 0)) * 2),
            scratch(4, most + 1, 8, width),
            dma((2,)),
            dma((STEPS + 1, 4)),
            dma((STEPS + 1, 4)),
            dma((3, 4, most)),
            dma((3, 4, most)),
            dma((4, 4, most, 2)),
            dma((4, 4, most, 2)),
            dma((4, most)),
            dma((4, most)),
        ],
        compiler_params=pltpu.CompilerParams(
            collective_id=0, has_side_effects=True, vmem_limit_bytes=62 * 2**20
        ),
        cost_estimate=pl.CostEstimate(
            flops=10 * n_rows * width * width, bytes_accessed=32 * 2**20, transcendentals=0
        ),
    )(field, conductivity, rate, ids, reservoir, weights, biases)
    state, share_w, bias_grad = out
    new_w, new_wm, new_wv = adam(weights, w_mom, w_var, share_w)
    position = lax.axis_index("gx") * gy_n + lax.axis_index("gy")
    share_b = lax.dynamic_slice_in_dim(bias_grad[:2], position * share, share, 1)
    new_b, new_bm, new_bv = adam(biases, b_mom, b_var, share_b)
    return (state, new_w, new_wm, new_wv, new_b, new_bm, new_bv)


def solution(mesh):
    return jax.shard_map(
        local,
        mesh=mesh,
        in_specs=(
            P(None, "gx", "gy"),
            P(None, "gx", "gy"),
            P(None, "gx", "gy"),
            P(("gx", "gy")),
            P(("gx", "gy"), None),
            P(("gx", "gy")),
            P(("gx", "gy"), None),
            P(None, ("gx", "gy"), None),
            P(None, ("gx", "gy"), None),
            P(None, ("gx", "gy"), None),
            P(None, ("gx", "gy")),
            P(None, ("gx", "gy")),
            P(None, ("gx", "gy")),
        ),
        out_specs=(
            P(None, "gx", "gy"),
            P(None, ("gx", "gy"), None),
            P(None, ("gx", "gy"), None),
            P(None, ("gx", "gy"), None),
            P(None, ("gx", "gy")),
            P(None, ("gx", "gy")),
            P(None, ("gx", "gy")),
        ),
        check_vma=False,
    )
```

```python
import functools

import jax
import jax.numpy as jnp
from jax import lax
from jax.experimental import pallas as pl
from jax.experimental.pallas import tpu as pltpu
from jax.sharding import PartitionSpec as P

PW = 32
STEPS = 4
TILE = 256

time_step = 0.15
learn_rate = 0.001
beta_one = 0.9
beta_two = 0.99
adam_count = 20
tiny_eps = 1e-08

MESH = pl.DeviceIdType.MESH
F32 = jnp.float32
BF16 = jnp.bfloat16


def adam(param, moment, second, grad):
    moment_new = beta_one * moment + (1.0 - beta_one) * grad
    second_new = beta_two * second + (1.0 - beta_two) * grad * grad
    mhat = moment_new / (1.0 - beta_one**adam_count)
    vhat = second_new / (1.0 - beta_two**adam_count)
    return (param - learn_rate * mhat / (jnp.sqrt(vhat) + tiny_eps), moment_new, second_new)


def dims_of(gx, gy):
    nx = max(1, gx // 4)
    return (gx // nx, nx, gy // 2, 2)


def kernel(
    gx_n,
    gy_n,
    field,
    cond,
    rate,
    ids,
    store,
    w,
    bias,
    new_field,
    grad_out,
    bias_grad,
    slot,
    cell,
    trainer,
    tiny,
    ua,
    ub,
    coef,
    cz,
    table,
    half,
    rows,
    counts,
    w0,
    w1,
    small,
    hid,
    gpb,
    g0,
    g1,
    brow,
    bsum,
    xsend,
    ysend,
    xrecv,
    yrecv,
    ycols,
    stages,
    bbuf,
    half_sem,
    hs_sem,
    hr_sem,
    ag_s,
    ag_r,
    rs_s,
    rs_r,
    bs_s,
    bs_r,
):
    dims = dims_of(gx_n, gy_n)
    nz, nx, ny, nc = dims
    gx, gy = lax.axis_index("gx"), lax.axis_index("gy")
    here = (gx // nx, lax.rem(gx, nx), gy // nc, lax.rem(gy, nc))
    depth, cx, cy = field.shape
    width = w.shape[2]
    hidb = half.at[pl.ds(0, rows.shape[0])]

    def loop(count, body, together):
        def several(q, carry):
            for j in range(together):
                body(q * together + j)
            return carry

        lax.fori_loop(0, count // together, several, 0)

    def device(axis, pos):
        p = list(here)
        p[axis] = pos
        return (p[0] * nx + p[1], p[2] * nc + p[3])

    barrier = pltpu.get_barrier_semaphore()
    for o in range(1, gx_n):
        pl.semaphore_signal(
            barrier, inc=1, device_id=(lax.rem(gx + o, gx_n), gy), device_id_type=MESH
        )
    for o in range(1, gy_n):
        pl.semaphore_signal(
            barrier, inc=1, device_id=(gx, lax.rem(gy + o, gy_n)), device_id_type=MESH
        )

    load = pltpu.make_async_copy(store.at[:, pl.ds(0, width)], half, half_sem.at[0])
    load.start()

    w0[here] = w[0].astype(w0.dtype)
    w1[here] = w[1].astype(w1.dtype)
    devices = gx_n * gy_n
    share = w.shape[1]
    upright = jnp.transpose(ids[...])
    place = 0
    for ref in (slot, cell, trainer):
        for g in range(ref.shape[0] // 128):
            ref[g * 128 : (g + 1) * 128, :] = jnp.broadcast_to(
                upright[:, place : place + 1], (128, 128)
            )
            place += 1
    lane = lax.broadcasted_iota(jnp.int32, trainer.shape, 1)
    hot_t = (trainer[...] == lane).astype(F32)
    tiny[...] = jnp.zeros_like(tiny)
    tiny[1:3, 0:share] = bias[...]
    sm = tiny[...]
    for i in range(1, 128 // share):
        sm = sm + pltpu.roll(tiny[...], share * i, 1)
    small[here] = sm
    small[(*here, pl.ds(0, 1))] = jnp.sum(hot_t, 0, keepdims=True)

    zero_x = jnp.zeros((depth, cy), F32)
    zero_y = jnp.zeros((cx, 128), F32)

    lanes = lax.broadcasted_iota(jnp.int32, (cx, cy), 1)
    subl = lax.broadcasted_iota(jnp.int32, (cx, cy), 0)

    def pack(index, plane):
        def several(q, acc):
            for j in range(8):
                z = q * 8 + j
                u = plane(z)
                xsend[index, 0, pl.ds(z, 1), :] = u[0:1, :]
                xsend[index, 1, pl.ds(z, 1), :] = u[cx - 1 : cx, :]
                ends = (lanes == 2 * z) | (lanes == lax.rem(2 * z + cy - 1, cy))
                acc = jnp.where(ends, pltpu.roll(u, 2 * z, 1), acc)
            return acc

        ysend[index] = lax.fori_loop(0, depth // 8, several, jnp.zeros((cx, cy), F32))

    def halo(index):
        out = []
        for side, (axis_pos, n, mk) in enumerate(
            (
                (gx, gx_n, lambda p: (p, gy)),
                (gx, gx_n, lambda p: (p, gy)),
                (gy, gy_n, lambda p: (gx, p)),
                (gy, gy_n, lambda p: (gx, p)),
            )
        ):
            up = side % 2 == 0
            sendbuf = (
                xsend.at[index, 1 if up else 0] if side < 2 else ysend.at[index]
            )
            recvbuf = (xrecv if side < 2 else yrecv).at[index, 0 if up else 1]
            peer = jnp.minimum(axis_pos + 1, n - 1) if up else jnp.maximum(axis_pos - 1, 0)
            copy = pltpu.make_async_remote_copy(
                src_ref=sendbuf,
                dst_ref=recvbuf,
                send_sem=hs_sem.at[index, side],
                recv_sem=hr_sem.at[index, side],
                device_id=mk(peer),
                device_id_type=MESH,
            )
            sends = axis_pos < n - 1 if up else axis_pos > 0
            gets = axis_pos > 0 if up else axis_pos < n - 1
            out.append((copy, sends, gets))
        return out

    def halo_start(index):
        for copy, sends, gets in halo(index):
            pl.when(sends)(copy.start)

    def halo_wait(index):
        for side, (copy, sends, gets) in enumerate(halo(index)):
            pl.when(sends)(copy.wait_send)
            pl.when(gets)(copy.wait_recv)
            buf = xrecv if side < 2 else yrecv

            @pl.when(jnp.logical_not(gets))
            def _():
                buf[index, side % 2] = zero_x if side < 2 else zero_y

        ycols[...] = jnp.where(
            lanes % 2 == 0, yrecv[index, 1], pltpu.roll(yrecv[index, 0], 2, 1)
        )

    def region(done, fixed=None):
        ind = []
        for a in range(4):
            if fixed is not None and a == fixed[0]:
                ind.append(fixed[1])
            else:
                ind.append(slice(None) if a in done else here[a])
        return tuple(ind)

    def gather(buf, order, which):
        done = []
        for phase, axis in enumerate(order):
            n = dims[axis]
            copies = []
            for o in range(1, n):
                ref = buf.at[region(done)]
                copy = pltpu.make_async_remote_copy(
                    src_ref=ref,
                    dst_ref=ref,
                    send_sem=ag_s.at[which, axis, o - 1],
                    recv_sem=ag_r.at[which, axis, o - 1],
                    device_id=device(axis, lax.rem(here[axis] + o, n)),
                    device_id_type=MESH,
                )
                copy.start()
                copies.append(copy)
            yield
            for copy in copies:
                copy.wait()
            done.append(axis)
            yield

    def step(gens):
        for g in gens:
            next(g, None)

    pl.semaphore_wait(barrier, gx_n - 1 + gy_n - 1)
    gens = [
        gather(small, (0, 1, 2, 3), 0),
        gather(w0, (0, 1, 2, 3), 1),
        gather(w1, (0, 2, 1, 3), 2),
    ]
    step(gens)
    pack(0, lambda z: cond[z])
    halo_start(0)
    pack(1, lambda z: field[z])
    halo_start(1)

    n_old = slot.shape[0]
    n_slots = store.shape[0]

    pick_tile = 512 if n_old % 1024 == 0 else TILE

    def pick(col, first, last):
        def one(t, carry):
            r = pl.ds(pl.multiple_of(t * pick_tile, pick_tile), pick_tile)
            hot = (
                slot[r, 0:1] == lax.broadcasted_iota(jnp.int32, (pick_tile, n_slots), 1)
            ).astype(F32).astype(BF16)
            rows[r, pl.ds(col, width)] = jnp.dot(
                hot, half[...], preferred_element_type=F32
            ).astype(BF16)
            return carry

        tiles = n_old // pick_tile
        lax.fori_loop(tiles * first // 2, tiles * last // 2, one, 0)

    def shifted(u, index, z):
        lo = xrecv[index, 0, pl.ds(z, 1), :]
        hi = xrecv[index, 1, pl.ds(z, 1), :]
        xm = jnp.where(subl == 0, lo, pltpu.roll(u, 1, 0))
        xp = jnp.where(subl == cx - 1, hi, pltpu.roll(u, cx - 1, 0))
        ends = pltpu.roll(ycols[...], cy - 1 - 2 * z, 1)
        ym = jnp.where(lanes == 0, ends, pltpu.roll(u, 1, 1))
        yp = jnp.where(lanes == cy - 1, ends, pltpu.roll(u, cy - 1, 1))
        return xm, xp, ym, yp

    half_step = 0.5 * time_step
    for buf in (ua, ub):
        buf[0] = jnp.zeros((cx, cy), F32)
        buf[depth + 1] = jnp.zeros((cx, cy), F32)
    cz[0] = half_step * cond[0]
    cz[depth] = half_step * cond[depth - 1]

    def z_coef(z):
        cz[z] = half_step * (cond[z - 1] + cond[z])
        ua[z] = field[z - 1]

    loop(depth - 1, lambda z: z_coef(z + 1), 1)
    ua[depth] = field[depth - 1]
    load.wait()
    pick(0, 0, 1)
    halo_wait(0)

    def make_coef(z):
        k = cond[z]
        total = time_step * rate[z] + cz[z] + cz[z + 1]
        for i, kn in enumerate(shifted(k, 0, z)):
            c = half_step * (k + kn)
            coef[i, z] = c
            total = total + c
        coef[4, z] = 1.0 - total

    loop(depth, make_coef, 4)

    def advance(index, src, dst):
        def one(z):
            u = src[z + 1]
            acc = coef[4, z] * u + cz[z] * src[z] + cz[z + 1] * src[z + 2]
            for i, un in enumerate(shifted(u, index, z)):
                acc = acc + coef[i, z] * un
            dst[z + 1] = acc

        loop(depth, one, 8)

    step(gens)
    step(gens)
    pick(0, 1, 2)
    load2 = pltpu.make_async_copy(store.at[:, pl.ds(width, width)], half, half_sem.at[1])
    load2.start()

    blocks = cy // PW
    per = 128 // PW
    group = lanes // PW

    def build(offset, plane):
        def one(q, carry):
            planes = [plane(q * per + j) for j in range(per)]
            for b in range(blocks):
                acc = None
                for j in range(per):
                    shift = (PW * (j - b)) % cy
                    v = planes[j] if shift == 0 else pltpu.roll(planes[j], shift, 1)
                    acc = v if acc is None else jnp.where(group == j, v, acc)
                table[
                    b * cx : (b + 1) * cx,
                    pl.ds(pl.multiple_of(offset + q * 128, 128), 128),
                ] = acc.astype(BF16)
            return carry

        lax.fori_loop(0, depth // per, one, 0)

    halo_wait(1)
    bufs = (ua, ub)
    for s in range(STEPS):
        src, dst = bufs[s % 2], bufs[(s + 1) % 2]
        advance(s + 1, src, dst)
        if s < STEPS - 1:
            pack(s + 2, lambda z: dst[z + 1])
            halo_start(s + 2)
            if s == 0:
                load2.wait()
                pick(width, 0, 1)
                step(gens)
                step(gens)
            if s == 1:
                pick(width, 1, 2)
            if s == 2:
                build(0, lambda z: field[z])
                step(gens)
                step(gens)
            halo_wait(s + 2)
    last = bufs[STEPS % 2]

    build(width, lambda z: last[z + 1])

    def emit(z):
        new_field[z] = last[z + 1]

    loop(depth, emit, 4)
    n_new = cell.shape[0]
    n_cells = table.shape[0]
    hot_c = (
        (cell[:, 0:1] == lax.broadcasted_iota(jnp.int32, (n_new, n_cells), 1))
        .astype(F32)
        .astype(BF16)
    )
    for c in range(0, 2 * width, 512):
        rows[n_old : n_old + n_new, c : c + 512] = jnp.dot(
            hot_c, table[:, c : c + 512], preferred_element_type=F32
        ).astype(BF16)

    step(gens)

    everyone = small[...].reshape(devices, 8, 128)
    totals = jnp.sum(everyone[:, 0, :], 0, keepdims=True) + float(n_old)
    position = gx * gy_n + gy
    lane1 = lax.broadcasted_iota(jnp.int32, (1, 128), 1)
    mine = jnp.sum(jnp.where(lane1 == position, totals, 0.0), 1, keepdims=True)
    counts[0:n_old, :] = jnp.broadcast_to(mine, (n_old, 128))
    counts[n_old : n_old + n_new, :] = jnp.broadcast_to(
        jnp.sum(hot_t * totals, 1, keepdims=True), (n_new, 128)
    )
    fit = 128 // share
    for layer in range(2):
        for j in range(width // 128):
            acc = jnp.zeros((1, 128), F32)
            for i in range(fit):
                acc = jnp.where(lane1 // share == i, everyone[j * fit + i, layer + 1 : layer + 2, :], acc)
            brow[layer : layer + 1, j * 128 : (j + 1) * 128] = acc.astype(BF16).astype(F32)

    n_rows = n_old + n_new
    tall = 640 if n_rows % 640 == 0 else TILE
    bsum[...] = jnp.zeros_like(bsum)

    def whole(ref):
        return ref[...].astype(BF16).reshape(width, width)

    def forward(t, carry):
        r = pl.ds(pl.multiple_of(t * tall, tall), tall)
        pre = jnp.dot(rows[r, :width], whole(w0), preferred_element_type=F32) + brow[0:1, :]
        h = jnp.tanh(pre)
        hid[r, :] = h
        hidb[r, :] = h.astype(BF16)
        return carry

    lax.fori_loop(0, n_rows // tall, forward, 0)

    def forward2(t, carry):
        r = pl.ds(pl.multiple_of(t * tall, tall), tall)
        pred = jnp.dot(hidb[r, :], whole(w1), preferred_element_type=F32) + brow[1:2, :]
        gp = 2.0 * (pred - rows[r, width : 2 * width].astype(F32)) / counts[r, 0:1]
        gpb[r, :] = gp.astype(BF16)
        bsum[1:2, :] += jnp.sum(gp, 0, keepdims=True)
        return carry

    lax.fori_loop(0, n_rows // tall, forward2, 0)

    coded = share % 16 == 0

    def each(left, body):
        count = 1
        for a in left:
            count *= dims[a]

        def one(i):
            ind, rest = [], i
            for a in reversed(left):
                ind.insert(0, lax.rem(rest, dims[a]))
                rest = rest // dims[a]
            full = list(here)
            for a, v in zip(left, ind):
                full[a] = v
            body(full, ind)

        if count <= 4:
            for i in range(count):
                one(i)
        else:
            loop(count, one, 4 if count % 4 == 0 else 1)

    def reduce(buf, piece, order):
        left = [0, 1, 2, 3]
        stage = stages[piece]
        cols = (slice(None), pl.ds(piece % 2 * (width // 2), width // 2))
        for phase, axis in enumerate(order):
            n = dims[axis]
            others = [a for a in left if a != axis]
            out, got, out_scale, got_scale = stage[phase]
            copies = []
            for o in range(1, n):
                peer = lax.rem(here[axis] + o, n)
                pairs = [(buf.at[(*region(left, (axis, peer)), *cols)], got.at[o - 1])]
                if coded:

                    def encode(full, ind):
                        full[axis] = peer
                        v = buf[(*full, *cols)]
                        top = jnp.max(jnp.abs(v), axis=0, keepdims=True)
                        top = jnp.maximum(jnp.max(top, axis=1, keepdims=True), 1e-30)
                        q = jnp.round(v * (32767.0 / top))
                        out[(o - 1, *ind)] = q.astype(jnp.int32).astype(jnp.int16)
                        out_scale[(o - 1, *ind)] = jnp.broadcast_to(top / 32767.0, (8, 128))

                    each(others, encode)
                    pairs = [
                        (out.at[o - 1], got.at[o - 1]),
                        (out_scale.at[o - 1], got_scale.at[o - 1]),
                    ]
                for part, (src, dst) in enumerate(pairs):
                    copy = pltpu.make_async_remote_copy(
                        src_ref=src,
                        dst_ref=dst,
                        send_sem=rs_s.at[piece, axis, o - 1, part],
                        recv_sem=rs_r.at[piece, axis, o - 1, part],
                        device_id=device(axis, peer),
                        device_id_type=MESH,
                    )
                    copy.start()
                    copies.append(copy)
            yield
            left.remove(axis)
            for copy in copies:
                copy.wait()

            def total(full, ind):
                acc = buf[(*full, *cols)]
                for o in range(n - 1):
                    v = got[(o, *ind)]
                    if coded:
                        v = v.astype(jnp.int32).astype(F32) * got_scale[(o, *ind)][0:1, 0:1]
                    acc = acc + v
                buf[(*full, *cols)] = acc

            each(left, total)
            yield

    def reduce_bias():
        for phase, axis in enumerate((3, 2, 1, 0)):
            n = dims[axis]
            copies = []
            for o in range(1, n):
                copy = pltpu.make_async_remote_copy(
                    src_ref=bbuf.at[axis, 0],
                    dst_ref=bbuf.at[axis, o],
                    send_sem=bs_s.at[axis, o - 1],
                    recv_sem=bs_r.at[axis, o - 1],
                    device_id=device(axis, lax.rem(here[axis] + o, n)),
                    device_id_type=MESH,
                )
                copy.start()
                copies.append(copy)
            yield
            for copy in copies:
                copy.wait()
            acc = bbuf[axis, 0]
            for o in range(1, n):
                acc = acc + bbuf[axis, o]
            if axis > 0:
                bbuf[axis - 1, 0] = acc
            else:
                bias_grad[...] = acc
            yield

    across = (((0,), (0,)), ((), ()))

    def store_grad(buf, col, value, start=0):
        per_tile = TILE // share
        flat = value.reshape(per_tile, share, value.shape[1])

        for i in range(per_tile):
            d = col * per_tile + i
            buf[
                d // (nx * ny * nc),
                lax.rem(d // (ny * nc), nx),
                lax.rem(d // nc, ny),
                lax.rem(d, nc),
                :,
                start : start + value.shape[1],
            ] = flat[i]

    def grad_two(j, carry):
        c = pl.ds(pl.multiple_of(j * TILE, TILE), TILE)
        store_grad(
            g1, j, lax.dot_general(hidb[:, c], gpb[...], across, preferred_element_type=F32)
        )
        return carry

    lax.fori_loop(0, width // TILE, grad_two, 0)
    layer1 = [reduce(g1, 2, (3, 1, 2, 0)), reduce(g1, 3, (3, 2, 1, 0))]
    layer0 = [reduce(g0, 0, (3, 1, 2, 0)), reduce(g0, 1, (3, 2, 1, 0))]

    def onward(pieces):
        for piece in pieces:
            step([piece, piece])

    step(layer1)

    def backward(t, carry):
        r = pl.ds(pl.multiple_of(t * tall, tall), tall)
        gh = lax.dot_general(
            gpb[r, :], whole(w1), (((1,), (1,)), ((), ())), preferred_element_type=F32
        )
        h = hid[r, :]
        ga = gh * (1.0 - h * h)
        hidb[r, :] = ga.astype(BF16)
        bsum[0:1, :] += jnp.sum(ga, 0, keepdims=True)
        return carry

    tiles = n_rows // tall
    lax.fori_loop(0, tiles // 2, backward, 0)
    onward(layer1)
    lax.fori_loop(tiles // 2, tiles, backward, 0)
    bbuf[3, 0] = bsum[...]
    redb = reduce_bias()
    next(redb)

    for h in range(2):
        start = h * (width // 2)

        def grad_one(j, carry):
            c = pl.ds(pl.multiple_of(j * TILE, TILE), TILE)
            part = lax.dot_general(
                rows[:, c],
                hidb[:, start : start + width // 2],
                across,
                preferred_element_type=F32,
            )
            store_grad(g0, j, part, start)
            return carry

        lax.fori_loop(0, width // TILE, grad_one, 0)
        step([layer0[h]])
        if h == 0:
            onward(layer1)
            onward([redb])
    onward(layer1)
    onward([redb])
    onward(layer0)
    onward([redb])
    onward(layer0)
    onward([redb])
    step(layer1)
    grad_out[1] = g1[here]
    onward(layer0)
    step(layer0)
    grad_out[0] = g0[here]


def local(
    field,
    conductivity,
    rate,
    patch_cell,
    trainer,
    res_slot,
    reservoir,
    weights,
    w_mom,
    w_var,
    biases,
    b_mom,
    b_var,
):
    gx_n, gy_n = lax.axis_size("gx"), lax.axis_size("gy")
    devices = gx_n * gy_n
    dims = dims_of(gx_n, gy_n)
    nz, nx, ny, nc = dims
    depth, cx, cy = field.shape
    share, width = weights.shape[1], weights.shape[2]
    blocks = cy // PW
    n_old, n_new = res_slot.shape[0], patch_cell.shape[0]
    n_rows = n_old + n_new
    cell = (patch_cell % blocks) * cx + patch_cell // blocks
    ids = jnp.concatenate([res_slot, cell, trainer[:, 0]]).reshape(-1, 128)
    ids = jnp.pad(ids, ((0, -ids.shape[0] % 8), (0, 0)))
    wire = BF16 if share % 16 == 0 else F32
    most = max(dims) - 1
    full = (*dims, share, width)
    vm = pl.BlockSpec(memory_space=pltpu.VMEM)

    def scratch(*shape, dtype=F32):
        return pltpu.VMEM(shape, dtype)

    coded = share % 16 == 0

    def stages(order):
        left, found = [0, 1, 2, 3], []
        for axis in order:
            left.remove(axis)
            shape = (dims[axis] - 1, *(dims[a] for a in left))
            body = (*shape, share, width // 2) if coded else (1,) * (len(shape) + 2)
            scale = (*shape, 8, 128) if coded else (1,) * (len(shape) + 2)
            kind = jnp.int16 if coded else F32
            found.append(
                (
                    scratch(*body, dtype=kind),
                    scratch(*shape, share, width // 2, dtype=kind),
                    scratch(*scale),
                    scratch(*scale),
                )
            )
        return tuple(found)

    dma = pltpu.SemaphoreType.DMA
    out = pl.pallas_call(
        functools.partial(kernel, gx_n, gy_n),
        out_shape=(
            jax.ShapeDtypeStruct(field.shape, F32),
            jax.ShapeDtypeStruct(weights.shape, F32),
            jax.ShapeDtypeStruct((8, width), F32),
        ),
        in_specs=[vm] * 4 + [pl.BlockSpec(memory_space=pl.ANY)] + [vm] * 2,
        out_specs=[vm] * 3,
        scratch_shapes=[
            scratch(n_old, 128, dtype=jnp.int32),
            scratch(n_new, 128, dtype=jnp.int32),
            scratch(n_new, 128, dtype=jnp.int32),
            scratch(8, 128),
            scratch(depth + 2, cx, cy),
            scratch(depth + 2, cx, cy),
            scratch(5, depth, cx, cy),
            scratch(depth + 1, cx, cy),
            scratch(blocks * cx, 2 * width, dtype=BF16),
            scratch(reservoir.shape[0], width, dtype=BF16),
            scratch(n_rows, 2 * width, dtype=BF16),
            scratch(n_rows, 128),
            scratch(*full, dtype=wire),
            scratch(*full, dtype=wire),
            scratch(*dims, 8, 128),
            scratch(n_rows, width),
            scratch(n_rows, width, dtype=BF16),
            scratch(*full),
            scratch(*full),
            scratch(8, width),
            scratch(8, width),
            scratch(STEPS + 1, 2, depth, cy),
            scratch(STEPS + 1, cx, cy),
            scratch(STEPS + 1, 2, depth, cy),
            scratch(STEPS + 1, 2, cx, cy),
            scratch(cx, cy),
            tuple(stages(order) for order in ((3, 1, 2, 0), (3, 2, 1, 0)) * 2),
            scratch(4, most + 1, 8, width),
            dma((2,)),
            dma((STEPS + 1, 4)),
            dma((STEPS + 1, 4)),
            dma((3, 4, most)),
            dma((3, 4, most)),
            dma((4, 4, most, 2)),
            dma((4, 4, most, 2)),
            dma((4, most)),
            dma((4, most)),
        ],
        compiler_params=pltpu.CompilerParams(
            collective_id=0, has_side_effects=True, vmem_limit_bytes=62 * 2**20
        ),
        cost_estimate=pl.CostEstimate(
            flops=10 * n_rows * width * width, bytes_accessed=32 * 2**20, transcendentals=0
        ),
    )(field, conductivity, rate, ids, reservoir, weights, biases)
    state, share_w, bias_grad = out
    new_w, new_wm, new_wv = adam(weights, w_mom, w_var, share_w)
    position = lax.axis_index("gx") * gy_n + lax.axis_index("gy")
    share_b = lax.dynamic_slice_in_dim(bias_grad[:2], position * share, share, 1)
    new_b, new_bm, new_bv = adam(biases, b_mom, b_var, share_b)
    return (state, new_w, new_wm, new_wv, new_b, new_bm, new_bv)


def solution(mesh):
    return jax.shard_map(
        local,
        mesh=mesh,
        in_specs=(
            P(None, "gx", "gy"),
            P(None, "gx", "gy"),
            P(None, "gx", "gy"),
            P(("gx", "gy")),
            P(("gx", "gy"), None),
            P(("gx", "gy")),
            P(("gx", "gy"), None),
            P(None, ("gx", "gy"), None),
            P(None, ("gx", "gy"), None),
            P(None, ("gx", "gy"), None),
            P(None, ("gx", "gy")),
            P(None, ("gx", "gy")),
            P(None, ("gx", "gy")),
        ),
        out_specs=(
            P(None, "gx", "gy"),
            P(None, ("gx", "gy"), None),
            P(None, ("gx", "gy"), None),
            P(None, ("gx", "gy"), None),
            P(None, ("gx", "gy")),
            P(None, ("gx", "gy")),
            P(None, ("gx", "gy")),
        ),
        check_vma=False,
    )
```
